128 devices in a mesh: lat: 4 (over z), lon: 32 (over x, y, core).
Axes of the slice: x: 4, y: 4, z: 4, core: 2. Of those that a mesh axis runs over, the one named last changes fastest.
Arguments:
- observations: float32 [1572864, 32], P(('lat', 'lon')), may hold values from -6 to 6
- destinations: int32 [1572864, 1], P(('lat', 'lon')), may hold values from 0 to 127; in each aligned block of 12288 rows (0 to 12287, 12288 to 24575, ...) at most 192 rows name the same one
- cells: int32 [1572864], P(('lat', 'lon')), may hold values from 0 to 1151
- first_weight: float32 [32, 256], replicated, may hold values from -1 to 1
- first_bias: float32 [256], replicated, may hold values from -3 to 3
- second_weight: bfloat16 [256, 256], replicated, may hold values from -0.375 to 0.375
- conv_first: bfloat16 [3, 3, 256, 256], replicated, may hold values from -0.125 to 0.125
- conv_bias: float32 [256], replicated, may hold values from -3 to 3
- conv_second: bfloat16 [3, 3, 256, 256], replicated, may hold values from -0.125 to 0.125
Outputs:
- encoded: bfloat16 [96, 1536, 256], P('lat', 'lon')
The draws below stay inside these ranges and needn't reach their ends.
Inputs may be any that keep to these rules, and one draw needn't show every extreme that they name: `destinations`: within the rows of one ingest shard, no tile is named by more than 192 rows, a bound that some block reaches.
All inputs are finite; a program needn't handle non-finite values.
Results may differ from the reference program's by a relative error of at most 0.015.
Values may be sent and summed in bfloat16 or wider, within the bound.
A program may use at most 128 MiB of HBM per device.

```python
import math
import jax
import jax.numpy as jnp
import numpy as np
from jax import lax

CHANNELS = 256
OBS_VALUES = 32
TILE_ROWS = 24
TILE_COLS = 48
OBS_DEV = 12288
CAP = 192
OBS_ROWS = 1572864
NLAT = 96
NLON = 1536
N_LAT = 4
N_LON = 32
DEVICES = 128


def touch_ends(result, own_key, low, top_value):
    index_at = [jax.random.randint(jax.random.fold_in(own_key, axis), (), 0, length) for axis, length in enumerate(result.shape)]
    main_axis = result.shape.index(max(result.shape))
    next_to = index_at[:main_axis] + [(index_at[main_axis] + 1) % result.shape[main_axis]] + index_at[main_axis + 1:]
    return result.at[tuple(index_at)].set(low).at[tuple(next_to)].set(top_value)


def block_levels(stream_key, shape, cuts, low, top_value):
    gain, own = 1.0, jax.random.fold_in(stream_key, 6)
    for axis_at, blocks in cuts:
        draws = jnp.exp(jax.random.uniform(jax.random.fold_in(own, axis_at), (blocks,), jnp.float32, low / len(cuts), top_value / len(cuts)))
        gain = gain * jnp.repeat(draws, shape[axis_at] // blocks).reshape([-1 if axis == axis_at else 1 for axis in range(len(shape))])
    return gain


def deal_out(rng, own, number, rows, number_of, top, bound, lean):
    sequence = jax.random.permutation(rng, number_of)
    crowded, ordinary = load_shares(number_of, rows * top, bound, lean, True), load_shares(number_of, rows * top, bound, lean, False)
    places = jnp.arange(number_of)

    def named(sizes, turn):
        used = int((sizes > 0).sum())
        fixed = max(1, used // 4)
        moved = fixed + (places - fixed + turn * (used - fixed)) % max(1, number_of - fixed)
        return jnp.zeros((number_of,), jnp.int32).at[sequence[jnp.where(places < fixed, places, moved)]].set(jnp.asarray(sizes, jnp.int32))

    sizes = jnp.where(number % 4 == 0, named(crowded, number // 4), named(ordinary, number - number // 4 - 1))
    mixed = jax.random.permutation(jax.random.fold_in(own, 3), number_of)
    source_of, sink = mixed[0:number_of // 2 * 2:2], mixed[1:number_of // 2 * 2:2]
    room = jnp.minimum(sizes[source_of] - 1, bound - sizes[sink]) // 2
    room = jnp.where((source_of == sequence[0]) | (sink == sequence[0]) | (sizes[sink] == 0), 0, jnp.maximum(room, 0))
    moved = jax.random.randint(jax.random.fold_in(own, 4), (number_of // 2,), 0, 1 << 20) % (room + 1)
    sizes = sizes.at[source_of].add(-moved).at[sink].add(moved)
    members = jnp.searchsorted(jnp.cumsum(sizes), jnp.arange(rows * top), side="right").astype(jnp.int32)
    table = members.reshape(top, rows).T
    table = table[jax.random.permutation(jax.random.fold_in(own, 1), rows)]
    turn = jax.random.randint(jax.random.fold_in(own, 2), (rows, 1), 0, top)
    return jnp.take_along_axis(table, (jnp.arange(top)[None, :] + turn) % top, axis=1)


def load_shares(amount, total, limit, lean, full):
    portions = [(1 << 20) // math.isqrt(rank ** lean) + 1 for rank in range(1, amount + 1)]
    largest = limit if full else min(limit, max(-(-total // amount), total * portions[0] // sum(portions)))
    least = 1 if total - largest >= amount - 1 else 0
    given, spare = [largest] + [least] * (amount - 1), total - largest - least * (amount - 1)
    while spare > 0:
        free = [i for i in range(1, amount) if given[i] < largest] or [i for i in range(1, amount) if given[i] < limit]
        mass, left = sum([portions[i] for i in free]), spare
        for i in free:
            more = min(limit - given[i], max(1, left * portions[i] // mass), spare)
            given[i] = given[i] + more
            spare = spare - more
    return np.array(given)


def scatter_about(rng, extent, scale, bound, pieces=(), dtype=jnp.bfloat16):
    factor_of = block_levels(rng, extent, pieces, -0.22, 0.18) if pieces else 1.0
    array = jax.random.normal(rng, extent, jnp.float32) * scale * factor_of
    return jnp.minimum(jnp.maximum(array, -bound), bound).astype(dtype)


def setup_inputs(seed: int = 0) -> dict:
    seeds = jax.random.split(jax.random.key(seed), 10)
    observations = scatter_about(seeds[0], (OBS_ROWS, OBS_VALUES), 1.0, 6.0, ((0, 128),), jnp.float32)
    destinations_keys = jax.random.split(jax.random.fold_in(seeds[1], 1), OBS_ROWS // OBS_DEV)
    destinations_turns = jax.random.permutation(jax.random.fold_in(seeds[1], 3), OBS_ROWS // OBS_DEV)
    destinations = jax.vmap(lambda own, number: deal_out(jax.random.fold_in(seeds[1], 2), own, number, OBS_DEV, DEVICES, 1, CAP, 2))(destinations_keys, destinations_turns).reshape((OBS_ROWS, 1))
    cells = touch_ends(jax.random.randint(seeds[2], (OBS_ROWS,), 0, TILE_ROWS * TILE_COLS), jax.random.fold_in(seeds[2], 1), 0, (TILE_ROWS * TILE_COLS) - 1).astype(jnp.int32)
    first_weight = scatter_about(seeds[3], (OBS_VALUES, CHANNELS), OBS_VALUES ** -0.5, 1.0, (), jnp.float32)
    first_bias = scatter_about(seeds[4], (CHANNELS,), 0.5, 3.0, (), jnp.float32)
    second_weight = scatter_about(seeds[5], (CHANNELS, CHANNELS), CHANNELS ** -0.5, 0.375)
    conv_first = scatter_about(seeds[6], (3, 3, CHANNELS, CHANNELS), (9 * CHANNELS) ** -0.5, 0.125)
    conv_bias = scatter_about(seeds[7], (CHANNELS,), 0.5, 3.0, (), jnp.float32)
    conv_second = scatter_about(seeds[8], (3, 3, CHANNELS, CHANNELS), (9 * CHANNELS) ** -0.5, 0.125)
    return {"observations": observations, "destinations": destinations, "cells": cells, "first_weight": first_weight, "first_bias": first_bias, "second_weight": second_weight, "conv_first": conv_first, "conv_bias": conv_bias, "conv_second": conv_second}


def encode_rows(rows, first_weight, first_bias, second_weight):
    pre = jnp.dot(rows, first_weight, precision=lax.Precision.HIGHEST, preferred_element_type=jnp.float32) + first_bias
    hidden = jax.nn.silu(pre).astype(jnp.bfloat16)
    return jnp.dot(hidden.astype(jnp.float32), second_weight.astype(jnp.float32), precision=lax.Precision.HIGHEST, preferred_element_type=jnp.float32).astype(jnp.bfloat16)


def convolve(field, kernel):
    half_turn = field.shape[1] // 2
    upper = jnp.roll(field[0], half_turn, axis=0)
    lower = jnp.roll(field[-1], half_turn, axis=0)
    padded = jnp.concatenate([upper[None], field, lower[None]], axis=0)
    padded = jnp.concatenate([padded[:, -1:], padded, padded[:, :1]], axis=1)
    rows_all = field.shape[0]
    cols_all = field.shape[1]
    width = field.shape[2]
    total = jnp.zeros((rows_all * cols_all, kernel.shape[3]), jnp.float32)
    for row_tap in range(3):
        for col_tap in range(3):
            window = padded[row_tap:row_tap + rows_all, col_tap:col_tap + cols_all].reshape(-1, width)
            total = total + jnp.dot(window.astype(jnp.float32), kernel[row_tap, col_tap].astype(jnp.float32), precision=lax.Precision.HIGHEST, preferred_element_type=jnp.float32)
    return total.reshape(rows_all, cols_all, -1)


def reference(observations, destinations, cells, first_weight, first_bias, second_weight, conv_first, conv_bias, conv_second):
    shards = N_LAT * N_LON
    grid_cells = NLAT * NLON
    obs_blocks = observations.reshape(shards, -1, OBS_VALUES)
    dest_blocks = destinations.reshape(shards, -1)
    cell_blocks = cells.reshape(shards, -1)

    def accumulate(carry, block):
        sums, counts = carry
        rows, tiles, spots = block
        band = tiles // N_LON
        sector = tiles % N_LON
        grid_row = band * TILE_ROWS + spots // TILE_COLS
        grid_col = sector * TILE_COLS + spots % TILE_COLS
        flat = (grid_row * NLON + grid_col).astype(jnp.int32)
        features = encode_rows(rows, first_weight, first_bias, second_weight)
        sums = sums + jax.ops.segment_sum(features.astype(jnp.float32), flat, num_segments=grid_cells)
        counts = counts + jax.ops.segment_sum(jnp.ones(flat.shape, jnp.float32), flat, num_segments=grid_cells)
        return (sums, counts), None

    start = (jnp.zeros((grid_cells, CHANNELS), jnp.float32), jnp.zeros((grid_cells,), jnp.float32))
    (sums, counts), _ = lax.scan(accumulate, start, (obs_blocks, dest_blocks, cell_blocks))
    latent = (sums / jnp.maximum(counts, 1.0)[:, None]).astype(jnp.bfloat16).reshape(NLAT, NLON, CHANNELS)
    middle = jax.nn.silu(convolve(latent, conv_first) + conv_bias).astype(jnp.bfloat16)
    return (latent.astype(jnp.float32) + convolve(middle, conv_second)).astype(jnp.bfloat16)
```

```python
import functools
import math

import jax
import jax.numpy as jnp
from jax import lax
from jax.experimental import pallas as pl
from jax.experimental.pallas import tpu as pltpu
from jax.sharding import PartitionSpec as P

TILE_ROWS = 24
TILE_COLS = 48
BLOCK = 256


def with_halo(cells, sides, width, closed):
    for axis, dim in sides:
        count = lax.axis_size(axis)
        ends = count if closed else count - 1
        head = lax.slice_in_dim(cells, 0, width, axis=dim)
        tail = lax.slice_in_dim(cells, cells.shape[dim] - width, cells.shape[dim], axis=dim)
        cells = jnp.concatenate(
            [
                lax.ppermute(tail, axis, [(i, (i + 1) % count) for i in range(ends)]),
                cells,
                lax.ppermute(head, axis, [((i + 1) % count, i) for i in range(ends)]),
            ],
            axis=dim,
        )
    return cells


def shifted(shard, axis, by):
    count = lax.axis_size(axis)
    return lax.ppermute(shard, axis, [(i, (i + by) % count) for i in range(count)])


def convolve(tile, kernel):
    padded = with_halo(tile, (("lat", 0),), 1, False)
    edges = jnp.stack([tile[0], tile[-1]])
    partner = shifted(edges, "lon", lax.axis_size("lon") // 2)
    band = lax.axis_index("lat")
    upper = jnp.where(band == 0, partner[0], padded[0])
    lower = jnp.where(band == lax.axis_size("lat") - 1, partner[1], padded[-1])
    padded = jnp.concatenate([upper[None], tile, lower[None]], axis=0)
    padded = with_halo(padded, (("lon", 1),), 1, True)
    tile_rows = tile.shape[0]
    tile_cols = tile.shape[1]
    width = tile.shape[2]
    total = jnp.zeros((tile_rows * tile_cols, kernel.shape[3]), jnp.float32)
    for row_tap in range(3):
        for col_tap in range(3):
            window = padded[row_tap : row_tap + tile_rows, col_tap : col_tap + tile_cols].reshape(
                -1, width
            )
            total = total + jnp.dot(
                window, kernel[row_tap, col_tap], preferred_element_type=jnp.float32
            )
    return total.reshape(tile_rows, tile_cols, -1)


def dispatch_kernel(shards, capacity, unroll, obs_ref, dest_ref, cell_ref, rows_ref, cells_ref,
                    source, slots, table, places, places_smem, copy_sem):
    values, count_rows = obs_ref.shape
    packing = 128 // values
    packed = capacity // packing
    planes = shards * packed
    blocks = count_rows // BLOCK
    f32, bf16, i32 = jnp.float32, jnp.bfloat16, jnp.int32

    lane = lax.broadcasted_iota(i32, (BLOCK, BLOCK + 128), 1)
    row = lax.broadcasted_iota(i32, (BLOCK, BLOCK + 128), 0)
    earlier = jnp.where((row < lane) | (lane >= BLOCK), 1.0, 0.0).astype(bf16)
    value_lane = lax.broadcasted_iota(i32, (values, 128), 1)
    value_row = lax.broadcasted_iota(i32, (values, 128), 0)
    spread = jnp.where(lax.rem(value_lane, values) == value_row, 1.0, 0.0).astype(bf16)
    tile_row = lax.broadcasted_iota(i32, (shards, BLOCK), 0)
    rank_row = lax.broadcasted_iota(i32, (capacity, BLOCK), 0).astype(f32)

    table[...] = jnp.zeros_like(table)

    def rank_block(block, carry):
        at = pl.multiple_of(block * BLOCK, BLOCK)
        dest = dest_ref[:, pl.ds(at, BLOCK)]
        cell = cell_ref[:, pl.ds(at, BLOCK)]
        named = jnp.where(tile_row == dest, 1.0, 0.0)
        counted = jnp.dot(named.astype(bf16), earlier, preferred_element_type=f32)
        before = counted[:, :BLOCK] + jnp.concatenate([carry] * (BLOCK // 128), axis=1)
        rank = jnp.sum(named * before, axis=0, keepdims=True)
        rank_whole = rank.astype(i32)
        plane = jnp.where(rank_whole >= packed, 1, 0)
        for cut in range(2, packing):
            plane = plane + jnp.where(rank_whole >= cut * packed, 1, 0)
        places[:, pl.ds(at, BLOCK)] = dest * packed + rank_whole + plane * (planes - packed)
        high = lax.shift_right_logical(cell, 6)
        low = cell - lax.shift_left(high, 6)
        weights = jnp.concatenate(
            [named * (high + 1).astype(f32), named * low.astype(f32)], axis=0
        ).astype(bf16)
        ranked = jnp.where(rank_row == rank, 1.0, 0.0).astype(bf16)
        table[...] += lax.dot_general(
            weights, ranked, (((1,), (1,)), ((), ())), preferred_element_type=f32
        )
        source[pl.ds(at, BLOCK), :] = lax.dot_general(
            obs_ref[:, pl.ds(at, BLOCK)].astype(bf16),
            spread,
            (((0,), (0,)), ((), ())),
            preferred_element_type=f32,
        )
        zero_at = pl.multiple_of(block * (packing * planes // blocks), 8)
        slots[pl.ds(zero_at, packing * planes // blocks), :] = jnp.zeros(
            (packing * planes // blocks, 128), f32
        )
        return carry + counted[:, BLOCK:]

    lax.fori_loop(0, blocks, rank_block, jnp.zeros((shards, 128), f32), unroll=4)

    copy = pltpu.make_async_copy(places, places_smem, copy_sem)
    copy.start()
    found = table[:shards, :].astype(i32) * 64 + table[shards:, :].astype(i32) - 64
    found = jnp.where(found >= 0, found, -1)
    absent = jnp.full((shards, 64), -1, i32)
    straight = jnp.concatenate([found, absent], axis=1)
    turned = jnp.concatenate([absent, found], axis=1)
    turn = lax.rem(lax.broadcasted_iota(i32, (shards, 1), 0) + lax.axis_index("lon"), 2)
    placed = jnp.where(turn == 1, turned, straight)
    cells_ref[:, 0, :] = placed[:, :128]
    cells_ref[:, 1, :] = placed[:, 128:]
    copy.wait()

    def move(step, _):
        at = pl.multiple_of(step * unroll, unroll)
        for k in range(unroll):
            place = places_smem[0, at + k]
            slots[pl.ds(place, 1), :] = source[pl.ds(at + k, 1), :]
        return 0

    lax.fori_loop(0, count_rows // unroll, move, 0)

    group = lax.broadcasted_iota(i32, (packed, 128), 1) // values

    def pack(dest, _):
        at = pl.multiple_of(dest * packed, packed)
        total = slots[pl.ds(at, packed), :]
        for plane in range(1, packing):
            total = jnp.where(group == plane, slots[pl.ds(plane * planes + at, packed), :], total)
        rows_ref[dest] = total.astype(bf16)
        return 0

    lax.fori_loop(0, shards, pack, 0, unroll=2)


def dispatch(obs, dest, cells, shards, capacity, unroll=64):
    count_rows, values = obs.shape
    packing = 128 // values
    packed = capacity // packing
    vmem = pl.BlockSpec(memory_space=pltpu.VMEM)
    return pl.pallas_call(
        functools.partial(dispatch_kernel, shards, capacity, unroll),
        out_shape=(
            jax.ShapeDtypeStruct((shards, packed, 128), jnp.bfloat16),
            jax.ShapeDtypeStruct((shards, 2, 128), jnp.int32),
        ),
        in_specs=[vmem] * 3,
        out_specs=[vmem] * 2,
        scratch_shapes=[
            pltpu.VMEM((count_rows, 128), jnp.float32),
            pltpu.VMEM((shards * capacity, 128), jnp.float32),
            pltpu.VMEM((2 * shards, capacity), jnp.float32),
            pltpu.VMEM((1, count_rows), jnp.int32),
            pltpu.SMEM((1, count_rows), jnp.int32),
            pltpu.SemaphoreType.DMA,
        ],
        compiler_params=pltpu.CompilerParams(vmem_limit_bytes=48 * 1024 * 1024),
        name="dispatch",
    )(obs.T, dest.reshape(1, -1), cells.reshape(1, -1))


def place_of(step, bands, sector_dims):
    digits = []
    for size in reversed(sector_dims):
        digits.append(lax.rem(step, size))
        step = lax.div(step, size)
    return step, digits[::-1]


def partner(step, sign, bands, sector_dims):
    band_step, steps = place_of(step, bands, sector_dims)
    _, mine = place_of(lax.axis_index("lon"), 1, sector_dims)
    band = lax.rem(lax.axis_index("lat") + (band_step if sign > 0 else bands - band_step), bands)
    sector = 0
    for size, digit, own in zip(sector_dims, steps, mine):
        sector = sector * size + lax.rem(own + (digit if sign > 0 else size - digit), size)
    return band, sector


def exchange_kernel(bands, sector_dims, group, chunk, rows_ref, cells_ref, first_ref, bias_ref, second_ref, latent_ref,
                    rows_got, cells_got, features, sums, counts, own_sem, send_rows, send_cells, recv_rows, recv_cells):
    shards, packed, _ = rows_got.shape
    values = first_ref.shape[0]
    width = second_ref.shape[1]
    packing = 128 // values
    capacity = packing * packed
    sectors = math.prod(sector_dims)
    tile_cells = TILE_ROWS * TILE_COLS
    f32, bf16, i32 = jnp.float32, jnp.bfloat16, jnp.int32
    mesh_id = pl.DeviceIdType.MESH

    barrier = pltpu.get_barrier_semaphore()

    def greet(step, _):
        pl.semaphore_signal(barrier, inc=1, device_id=partner(step, 1, bands, sector_dims), device_id_type=mesh_id)
        return 0

    lax.fori_loop(1, shards, greet, 0)
    pl.semaphore_wait(barrier, shards - 1)

    def copies(step):
        band, sector = partner(step, 1, bands, sector_dims)
        target = band * sectors + sector
        return (
            pltpu.make_async_remote_copy(
                src_ref=rows_ref.at[target], dst_ref=rows_got.at[step], send_sem=send_rows.at[step],
                recv_sem=recv_rows.at[step], device_id=(band, sector), device_id_type=mesh_id),
            pltpu.make_async_remote_copy(
                src_ref=cells_ref.at[target], dst_ref=cells_got.at[step], send_sem=send_cells.at[step],
                recv_sem=recv_cells.at[step], device_id=(band, sector), device_id_type=mesh_id),
        )

    def send(step, _):
        for copy in copies(step):
            copy.start()
        return 0

    me = lax.axis_index("lat") * sectors + lax.axis_index("lon")
    own_rows = pltpu.make_async_copy(rows_ref.at[me], rows_got.at[0], own_sem.at[0])
    own_cells = pltpu.make_async_copy(cells_ref.at[me], cells_got.at[0], own_sem.at[1])
    own_rows.start()
    own_cells.start()
    lax.fori_loop(1, shards, send, 0)

    sums[...] = jnp.zeros_like(sums)
    counts[...] = jnp.zeros_like(counts)
    first = first_ref[...]
    first_high = first.astype(bf16)
    first_low = (first - first_high.astype(f32)).astype(bf16)
    blank = jnp.zeros((values, width), bf16)
    weights = []
    for plane in range(packing):
        pieces = [blank] * (2 * packing)
        pieces[plane] = first_high
        pieces[packing + plane] = first_low
        weights.append(jnp.concatenate(pieces, axis=0))
    half_bias = 0.5 * bias_ref[...]
    own_rows.wait()
    own_cells.wait()

    lane = lax.broadcasted_iota(i32, (1, 128), 1)

    def receive(step, _):
        for copy in copies(step):
            copy.wait_recv()
        return 0

    def work(number, _):
        base = number * group
        lax.fori_loop(jnp.maximum(base, 1), base + group, receive, 0)
        rows = rows_got[pl.ds(base, group)].reshape(group * packed, 128)
        rows = jnp.concatenate([rows, rows], axis=1)
        for plane in range(packing):
            half = 0.5 * jnp.dot(rows, weights[plane], preferred_element_type=f32) + half_bias
            hidden = (half + half * jnp.tanh(half)).astype(bf16)
            made = jnp.dot(hidden, second_ref[...], preferred_element_type=f32).astype(bf16)
            features[:, plane] = made.reshape(group, packed, width)
        for part in range(group // chunk):
            pieces = []
            for pair in range(part * chunk // 2, (part + 1) * chunk // 2):
                even = cells_got[base + 2 * pair]
                odd = cells_got[base + 2 * pair + 1]
                pieces += [even[0:1], jnp.where(lane < 64, even[1:2], odd[0:1]), odd[1:2]]
            cell = jnp.concatenate(pieces, axis=1)
            span = chunk * capacity
            spots = lax.broadcasted_iota(jnp.int16, (tile_cells, span), 0)
            onehot = jnp.where(spots == cell.astype(jnp.int16), 1.0, 0.0).astype(bf16)
            sums[...] += jnp.dot(
                onehot, features[pl.ds(part * chunk, chunk)].reshape(span, width), preferred_element_type=f32)
            line = lax.shift_right_arithmetic(cell * 1366, 16)
            column = cell - line * TILE_COLS
            lines = jnp.where(lax.broadcasted_iota(i32, (32, span), 0) == line, 1.0, 0.0).astype(bf16)
            columns = jnp.where(
                (lax.broadcasted_iota(i32, (TILE_COLS, span), 0) == column) & (cell >= 0), 1.0, 0.0).astype(bf16)
            counts[...] += lax.dot_general(columns, lines, (((1,), (1,)), ((), ())), preferred_element_type=f32)
        return 0

    lax.fori_loop(0, shards // group, work, 0)

    scale = 1.0 / jnp.maximum(counts[...], 1.0)
    for line in range(TILE_ROWS):
        block = sums[pl.ds(line * TILE_COLS, TILE_COLS), :] * scale[:, line:line + 1]
        latent_ref[line] = block.astype(bf16)

    def drain(step, _):
        for copy in copies(step):
            copy.wait_send()
        return 0

    lax.fori_loop(1, shards, drain, 0)


def exchange(rows, cells, first_weight, first_bias, second_weight, bands, sector_dims, group=16, chunk=4):
    shards, packed, _ = rows.shape
    width = second_weight.shape[1]
    vmem = pl.BlockSpec(memory_space=pltpu.VMEM)
    anywhere = pl.BlockSpec(memory_space=pl.ANY)
    packing = 128 // first_weight.shape[0]
    dma = pltpu.SemaphoreType.DMA
    return pl.pallas_call(
        functools.partial(exchange_kernel, bands, sector_dims, group, chunk),
        out_shape=jax.ShapeDtypeStruct((TILE_ROWS, TILE_COLS, width), jnp.bfloat16),
        in_specs=[anywhere, anywhere, vmem, vmem, vmem],
        out_specs=vmem,
        scratch_shapes=[
            pltpu.VMEM((shards, packed, 128), jnp.bfloat16),
            pltpu.VMEM((shards, 2, 128), jnp.int32),
            pltpu.VMEM((group, packing, packed, width), jnp.bfloat16),
            pltpu.VMEM((TILE_ROWS * TILE_COLS, width), jnp.float32),
            pltpu.VMEM((TILE_COLS, 32), jnp.float32),
            dma((2,)), dma((shards,)), dma((shards,)), dma((shards,)), dma((shards,)),
        ],
        compiler_params=pltpu.CompilerParams(
            collective_id=0, has_side_effects=True, vmem_limit_bytes=48 * 1024 * 1024),
        name="exchange",
    )(rows, cells, first_weight, first_bias.reshape(1, -1), second_weight)


def body(
    observations,
    destinations,
    cells,
    first_weight,
    first_bias,
    second_weight,
    conv_first,
    conv_bias,
    conv_second,
):
    bands = lax.axis_size("lat")
    sectors = lax.axis_size("lon")
    shards = bands * sectors
    capacity = 2 * observations.shape[0] // shards
    rows, spots = dispatch(observations, destinations, cells, shards, capacity)
    latent = exchange(rows, spots, first_weight, first_bias, second_weight, bands, (4, 4, 2))
    middle = jax.nn.silu(convolve(latent, conv_first) + conv_bias).astype(jnp.bfloat16)
    return (latent.astype(jnp.float32) + convolve(middle, conv_second)).astype(jnp.bfloat16)


def solution(mesh):
    in_specs = (
        P(("lat", "lon"), None),
        P(("lat", "lon"), None),
        P(("lat", "lon")),
        P(),
        P(),
        P(),
        P(),
        P(),
        P(),
    )
    out_specs = P("lat", "lon", None)
    return jax.shard_map(body, mesh=mesh, in_specs=in_specs, out_specs=out_specs, check_vma=False)
```

```python
import functools
import math

import jax
import jax.numpy as jnp
from jax import lax
from jax.experimental import pallas as pl
from jax.experimental.pallas import tpu as pltpu
from jax.sharding import PartitionSpec as P

TILE_ROWS = 24
TILE_COLS = 48
BLOCK = 256


def dispatch_kernel(shards, capacity, unroll, obs_ref, dest_ref, cell_ref, rows_ref, cells_ref,
                    source, slots, table, places, places_smem, copy_sem):
    values, count_rows = obs_ref.shape
    packing = 128 // values
    packed = capacity // packing
    planes = shards * packed
    blocks = count_rows // BLOCK
    f32, bf16, i32 = jnp.float32, jnp.bfloat16, jnp.int32

    lane = lax.broadcasted_iota(i32, (BLOCK, BLOCK + 128), 1)
    row = lax.broadcasted_iota(i32, (BLOCK, BLOCK + 128), 0)
    earlier = jnp.where((row < lane) | (lane >= BLOCK), 1.0, 0.0).astype(bf16)
    value_lane = lax.broadcasted_iota(i32, (values, 128), 1)
    value_row = lax.broadcasted_iota(i32, (values, 128), 0)
    spread = jnp.where(lax.rem(value_lane, values) == value_row, 1.0, 0.0).astype(bf16)
    tile_row = lax.broadcasted_iota(i32, (shards, BLOCK), 0)
    rank_row = lax.broadcasted_iota(i32, (capacity, BLOCK), 0).astype(f32)

    table[...] = jnp.zeros_like(table)

    def rank_block(block, carry):
        at = pl.multiple_of(block * BLOCK, BLOCK)
        dest = dest_ref[:, pl.ds(at, BLOCK)]
        cell = cell_ref[:, pl.ds(at, BLOCK)]
        named = jnp.where(tile_row == dest, 1.0, 0.0)
        counted = jnp.dot(named.astype(bf16), earlier, preferred_element_type=f32)
        before = counted[:, :BLOCK] + jnp.concatenate([carry] * (BLOCK // 128), axis=1)
        rank = jnp.sum(named * before, axis=0, keepdims=True)
        rank_whole = rank.astype(i32)
        plane = jnp.where(rank_whole >= packed, 1, 0)
        for cut in range(2, packing):
            plane = plane + jnp.where(rank_whole >= cut * packed, 1, 0)
        places[:, pl.ds(at, BLOCK)] = dest * packed + rank_whole + plane * (planes - packed)
        high = lax.shift_right_logical(cell, 6)
        low = cell - lax.shift_left(high, 6)
        weights = jnp.concatenate(
            [named * (high + 1).astype(f32), named * low.astype(f32)], axis=0
        ).astype(bf16)
        ranked = jnp.where(rank_row == rank, 1.0, 0.0).astype(bf16)
        table[...] += lax.dot_general(
            weights, ranked, (((1,), (1,)), ((), ())), preferred_element_type=f32
        )
        source[pl.ds(at, BLOCK), :] = lax.dot_general(
            obs_ref[:, pl.ds(at, BLOCK)].astype(bf16),
            spread,
            (((0,), (0,)), ((), ())),
            preferred_element_type=f32,
        )
        zero_at = pl.multiple_of(block * (packing * planes // blocks), 8)
        slots[pl.ds(zero_at, packing * planes // blocks), :] = jnp.zeros(
            (packing * planes // blocks, 128), f32
        )
        return carry + counted[:, BLOCK:]

    lax.fori_loop(0, blocks, rank_block, jnp.zeros((shards, 128), f32), unroll=4)

    copy = pltpu.make_async_copy(places, places_smem, copy_sem)
    copy.start()
    found = table[:shards, :].astype(i32) * 64 + table[shards:, :].astype(i32) - 64
    found = jnp.where(found >= 0, found, -1)
    absent = jnp.full((shards, 64), -1, i32)
    straight = jnp.concatenate([found, absent], axis=1)
    turned = jnp.concatenate([absent, found], axis=1)
    turn = lax.rem(lax.broadcasted_iota(i32, (shards, 1), 0) + lax.axis_index("lon"), 2)
    placed = jnp.where(turn == 1, turned, straight)
    cells_ref[:, 0, :] = placed[:, :128]
    cells_ref[:, 1, :] = placed[:, 128:]
    copy.wait()

    def move(step, _):
        at = pl.multiple_of(step * unroll, unroll)
        for k in range(unroll):
            place = places_smem[0, at + k]
            slots[pl.ds(place, 1), :] = source[pl.ds(at + k, 1), :]
        return 0

    lax.fori_loop(0, count_rows // unroll, move, 0)

    group = lax.broadcasted_iota(i32, (packed, 128), 1) // values

    def pack(dest, _):
        at = pl.multiple_of(dest * packed, packed)
        total = slots[pl.ds(at, packed), :]
        for plane in range(1, packing):
            total = jnp.where(group == plane, slots[pl.ds(plane * planes + at, packed), :], total)
        rows_ref[dest] = total.astype(bf16)
        return 0

    lax.fori_loop(0, shards, pack, 0, unroll=2)


def dispatch(obs, dest, cells, shards, capacity, unroll=64):
    count_rows, values = obs.shape
    packing = 128 // values
    packed = capacity // packing
    vmem = pl.BlockSpec(memory_space=pltpu.VMEM)
    return pl.pallas_call(
        functools.partial(dispatch_kernel, shards, capacity, unroll),
        out_shape=(
            jax.ShapeDtypeStruct((shards, packed, 128), jnp.bfloat16),
            jax.ShapeDtypeStruct((shards, 2, 128), jnp.int32),
        ),
        in_specs=[vmem] * 3,
        out_specs=[vmem] * 2,
        scratch_shapes=[
            pltpu.VMEM((count_rows, 128), jnp.float32),
            pltpu.VMEM((shards * capacity, 128), jnp.float32),
            pltpu.VMEM((2 * shards, capacity), jnp.float32),
            pltpu.VMEM((1, count_rows), jnp.int32),
            pltpu.SMEM((1, count_rows), jnp.int32),
            pltpu.SemaphoreType.DMA,
        ],
        compiler_params=pltpu.CompilerParams(vmem_limit_bytes=48 * 1024 * 1024),
        name="dispatch",
    )(obs.T, dest.reshape(1, -1), cells.reshape(1, -1))


PITCH = 64


def encode_tile(sums, scale, first_kernel, second_kernel, bias_ref, out_ref, field, shifted, middle,
                row_edges, column_edges, corner_edges, row_halos, column_halos, corner_halos,
                send_halo, recv_halo):
    f32, bf16, i32 = jnp.float32, jnp.bfloat16, jnp.int32
    mesh_id = pl.DeviceIdType.MESH
    bands, sectors = lax.axis_size("lat"), lax.axis_size("lon")
    band, sector = lax.axis_index("lat"), lax.axis_index("lon")
    width = sums.shape[1]

    def at(line, column):
        return (line + 3) * PITCH + column

    for line in range(TILE_ROWS):
        block = sums[pl.ds(line * TILE_COLS, TILE_COLS), :] * scale[:, line:line + 1]
        block = block.astype(bf16)
        field[pl.ds(at(line, 0), TILE_COLS), :] = block.astype(f32)
        if line < 2:
            row_edges[0, line] = block
        if line >= TILE_ROWS - 2:
            row_edges[1, TILE_ROWS - 1 - line] = block
    for side, columns in enumerate(((0, 1), (TILE_COLS - 1, TILE_COLS - 2))):
        for depth, column in enumerate(columns):
            for line in range(TILE_ROWS):
                column_edges[side, depth, pl.ds(line, 1), :] = field[pl.ds(at(line, column), 1), :]
        for end, lines in enumerate(((0, 1), (TILE_ROWS - 1, TILE_ROWS - 2))):
            for i, line in enumerate(lines):
                for j, column in enumerate(columns):
                    corner_edges[end, side, pl.ds(2 * i + j, 1), :] = field[pl.ds(at(line, column), 1), :]

    north = band > 0
    south = band < bands - 1
    vertical = (
        (jnp.where(north, band - 1, 0), jnp.where(north, 0, sectors // 2), jnp.where(north, 1, 0)),
        (jnp.where(south, band + 1, bands - 1), jnp.where(south, 0, sectors // 2), jnp.where(south, 0, 1)),
    )
    copies = []

    def ship(source, target, slot, target_band, shift):
        copies.append(
            pltpu.make_async_remote_copy(
                src_ref=source, dst_ref=target, send_sem=send_halo.at[len(copies)], recv_sem=recv_halo.at[slot],
                device_id=(target_band, lax.rem(sector + shift + 2 * sectors, sectors)), device_id_type=mesh_id))
        copies[-1].start()

    for end, (target_band, shift, landing) in enumerate(vertical):
        ship(row_edges.at[end], row_halos.at[landing], landing, target_band, shift)
    for side, step in enumerate((-1, 1)):
        ship(column_edges.at[side], column_halos.at[1 - side], 2 + 1 - side, band, step)
    for end, (target_band, shift, landing) in enumerate(vertical):
        for side, step in enumerate((-1, 1)):
            ship(corner_edges.at[end, side], corner_halos.at[landing, 1 - side], 4 + 2 * landing + 1 - side,
                 target_band, shift + step)
    arrivals = [row_halos.at[0], row_halos.at[1], column_halos.at[0], column_halos.at[1]]
    arrivals += [corner_halos.at[end, side] for end in range(2) for side in range(2)]
    for slot, buffer in enumerate(arrivals):
        pltpu.make_async_remote_copy(
            src_ref=buffer, dst_ref=buffer, send_sem=send_halo.at[slot], recv_sem=recv_halo.at[slot],
            device_id=(band, sector), device_id_type=mesh_id).wait_recv()

    for end, lines in enumerate(((-1, -2), (TILE_ROWS, TILE_ROWS + 1))):
        for depth, line in enumerate(lines):
            field[pl.ds(at(line, 0), TILE_COLS), :] = row_halos[end, depth].astype(f32)
    for side, columns in enumerate(((-1, -2), (TILE_COLS, TILE_COLS + 1))):
        for depth, column in enumerate(columns):
            for line in range(TILE_ROWS):
                field[pl.ds(at(line, column), 1), :] = column_halos[side, depth, pl.ds(line, 1), :]
        for end, lines in enumerate(((-1, -2), (TILE_ROWS, TILE_ROWS + 1))):
            for i, line in enumerate(lines):
                for j, column in enumerate(columns):
                    field[pl.ds(at(line, column), 1), :] = corner_halos[end, side, pl.ds(2 * i + j, 1), :]

    def spread(array, start, stop):
        for tap in range(3):
            shifted[pl.ds(start, stop - start), tap * width:(tap + 1) * width] = (
                array[pl.ds(start + tap - 1, stop - start), :].astype(bf16))

    low, high = at(-1, -16), at(TILE_ROWS, PITCH)
    spread(field, low - PITCH, high + PITCH)
    total = 0.0
    for tap in range(3):
        total += jnp.dot(shifted[pl.ds(low + (tap - 1) * PITCH, high - low), :], first_kernel[tap],
                         preferred_element_type=f32)
    tall = PITCH + 16
    turned = 0.0
    for tap in range(3):
        lines = jnp.concatenate(
            [shifted[pl.ds(at(line - (tap - 1), -16), tall), :] for line in (-1, TILE_ROWS)], axis=0)
        turned += jnp.dot(lines, first_kernel[tap], preferred_element_type=f32)
    half_bias = 0.5 * bias_ref[...]

    def activate(value):
        half = 0.5 * value + half_bias
        return half + half * jnp.tanh(half)

    middle[pl.ds(low, high - low), :] = activate(total)
    turned = activate(turned)
    spot = lax.broadcasted_iota(i32, (tall, width), 0)
    inside = (spot >= 15) & (spot < 16 + TILE_COLS + 1)
    for index, (line, polar) in enumerate(((-1, band == 0), (TILE_ROWS, band == bands - 1))):
        place = pl.ds(at(line, -16), tall)
        chosen = jnp.where(polar, 1, 0)
        middle[place, :] = jnp.where(
            inside & (chosen == 1), turned[index * tall:(index + 1) * tall], middle[place, :])

    start, stop = at(0, 0), at(TILE_ROWS, 0)
    spread(middle, start - PITCH, stop + PITCH)
    total = field[pl.ds(start, stop - start), :]
    for tap in range(3):
        total += jnp.dot(shifted[pl.ds(start + (tap - 1) * PITCH, stop - start), :], second_kernel[tap],
                         preferred_element_type=f32)
    out_ref[...] = total.reshape(TILE_ROWS, PITCH, width)[:, :TILE_COLS].astype(bf16)
    for copy in copies:
        copy.wait_send()


def place_of(step, bands, sector_dims):
    digits = []
    for size in reversed(sector_dims):
        digits.append(lax.rem(step, size))
        step = lax.div(step, size)
    return step, digits[::-1]


def partner(step, sign, bands, sector_dims):
    band_step, steps = place_of(step, bands, sector_dims)
    _, mine = place_of(lax.axis_index("lon"), 1, sector_dims)
    band = lax.rem(lax.axis_index("lat") + (band_step if sign > 0 else bands - band_step), bands)
    sector = 0
    for size, digit, own in zip(sector_dims, steps, mine):
        sector = sector * size + lax.rem(own + (digit if sign > 0 else size - digit), size)
    return band, sector


def exchange_kernel(bands, sector_dims, group, chunk, rows_ref, cells_ref, first_ref, bias_ref, second_ref,
                    conv_first_ref, conv_bias_ref, conv_second_ref, out_ref,
                    rows_got, cells_got, features, sums, counts, first_kernel, second_kernel, field, shifted, middle,
                    row_edges, column_edges, corner_edges, row_halos, column_halos, corner_halos, own_sem, send_rows, send_cells, recv_rows, recv_cells,
                    send_halo, recv_halo):
    shards, packed, _ = rows_got.shape
    values = first_ref.shape[0]
    width = second_ref.shape[1]
    packing = 128 // values
    capacity = packing * packed
    sectors = math.prod(sector_dims)
    tile_cells = TILE_ROWS * TILE_COLS
    f32, bf16, i32 = jnp.float32, jnp.bfloat16, jnp.int32
    mesh_id = pl.DeviceIdType.MESH

    barrier = pltpu.get_barrier_semaphore()

    def greet(step, _):
        pl.semaphore_signal(barrier, inc=1, device_id=partner(step, 1, bands, sector_dims), device_id_type=mesh_id)
        return 0

    lax.fori_loop(1, shards, greet, 0)
    pl.semaphore_wait(barrier, shards - 1)

    def copies(step):
        band, sector = partner(step, 1, bands, sector_dims)
        target = band * sectors + sector
        return (
            pltpu.make_async_remote_copy(
                src_ref=rows_ref.at[target], dst_ref=rows_got.at[step], send_sem=send_rows.at[step],
                recv_sem=recv_rows.at[step], device_id=(band, sector), device_id_type=mesh_id),
            pltpu.make_async_remote_copy(
                src_ref=cells_ref.at[target], dst_ref=cells_got.at[step], send_sem=send_cells.at[step],
                recv_sem=recv_cells.at[step], device_id=(band, sector), device_id_type=mesh_id),
        )

    def send(step, _):
        for copy in copies(step):
            copy.start()
        return 0

    me = lax.axis_index("lat") * sectors + lax.axis_index("lon")
    own_rows = pltpu.make_async_copy(rows_ref.at[me], rows_got.at[0], own_sem.at[0])
    own_cells = pltpu.make_async_copy(cells_ref.at[me], cells_got.at[0], own_sem.at[1])
    own_rows.start()
    own_cells.start()
    kernels = [
        pltpu.make_async_copy(conv_first_ref, first_kernel, own_sem.at[2]),
        pltpu.make_async_copy(conv_second_ref, second_kernel, own_sem.at[3]),
    ]
    for copy in kernels:
        copy.start()
    lax.fori_loop(1, shards, send, 0)

    sums[...] = jnp.zeros_like(sums)
    counts[...] = jnp.zeros_like(counts)
    first = first_ref[...]
    first_high = first.astype(bf16)
    first_low = (first - first_high.astype(f32)).astype(bf16)
    blank = jnp.zeros((values, width), bf16)
    weights = []
    for plane in range(packing):
        pieces = [blank] * (2 * packing)
        pieces[plane] = first_high
        pieces[packing + plane] = first_low
        weights.append(jnp.concatenate(pieces, axis=0))
    half_bias = 0.5 * bias_ref[...]
    own_rows.wait()
    own_cells.wait()

    lane = lax.broadcasted_iota(i32, (1, 128), 1)

    def receive(step, _):
        for copy in copies(step):
            copy.wait_recv()
        return 0

    def work(number, _):
        base = number * group
        lax.fori_loop(jnp.maximum(base, 1), base + group, receive, 0)
        rows = rows_got[pl.ds(base, group)].reshape(group * packed, 128)
        rows = jnp.concatenate([rows, rows], axis=1)
        for plane in range(packing):
            half = 0.5 * jnp.dot(rows, weights[plane], preferred_element_type=f32) + half_bias
            hidden = (half + half * jnp.tanh(half)).astype(bf16)
            made = jnp.dot(hidden, second_ref[...], preferred_element_type=f32).astype(bf16)
            features[:, plane] = made.reshape(group, packed, width)
        for part in range(group // chunk):
            pieces = []
            for pair in range(part * chunk // 2, (part + 1) * chunk // 2):
                even = cells_got[base + 2 * pair]
                odd = cells_got[base + 2 * pair + 1]
                pieces += [even[0:1], jnp.where(lane < 64, even[1:2], odd[0:1]), odd[1:2]]
            cell = jnp.concatenate(pieces, axis=1)
            span = chunk * capacity
            spots = lax.broadcasted_iota(jnp.int16, (tile_cells, span), 0)
            onehot = jnp.where(spots == cell.astype(jnp.int16), 1.0, 0.0).astype(bf16)
            sums[...] += jnp.dot(
                onehot, features[pl.ds(part * chunk, chunk)].reshape(span, width), preferred_element_type=f32)
            line = lax.shift_right_arithmetic(cell * 1366, 16)
            column = cell - line * TILE_COLS
            lines = jnp.where(lax.broadcasted_iota(i32, (32, span), 0) == line, 1.0, 0.0).astype(bf16)
            columns = jnp.where(
                (lax.broadcasted_iota(i32, (TILE_COLS, span), 0) == column) & (cell >= 0), 1.0, 0.0).astype(bf16)
            counts[...] += lax.dot_general(columns, lines, (((1,), (1,)), ((), ())), preferred_element_type=f32)
        return 0

    lax.fori_loop(0, shards // group, work, 0)

    scale = 1.0 / jnp.maximum(counts[...], 1.0)
    for copy in kernels:
        copy.wait()
    encode_tile(sums, scale, first_kernel, second_kernel, conv_bias_ref, out_ref, field, shifted, middle,
                row_edges, column_edges, corner_edges, row_halos, column_halos, corner_halos, send_halo, recv_halo)

    def drain(step, _):
        for copy in copies(step):
            copy.wait_send()
        return 0

    lax.fori_loop(1, shards, drain, 0)


def exchange(rows, cells, first_weight, first_bias, second_weight, conv_first, conv_bias, conv_second, bands, sector_dims, group=16, chunk=4):
    shards, packed, _ = rows.shape
    width = second_weight.shape[1]
    vmem = pl.BlockSpec(memory_space=pltpu.VMEM)
    anywhere = pl.BlockSpec(memory_space=pl.ANY)
    packing = 128 // first_weight.shape[0]
    dma = pltpu.SemaphoreType.DMA
    field_rows = (TILE_ROWS + 5) * PITCH + 16
    return pl.pallas_call(
        functools.partial(exchange_kernel, bands, sector_dims, group, chunk),
        out_shape=jax.ShapeDtypeStruct((TILE_ROWS, TILE_COLS, width), jnp.bfloat16),
        in_specs=[anywhere, anywhere, vmem, vmem, vmem, anywhere, vmem, anywhere],
        out_specs=vmem,
        scratch_shapes=[
            pltpu.VMEM((shards, packed, 128), jnp.bfloat16),
            pltpu.VMEM((shards, 2, 128), jnp.int32),
            pltpu.VMEM((group, packing, packed, width), jnp.bfloat16),
            pltpu.VMEM((TILE_ROWS * TILE_COLS, width), jnp.float32),
            pltpu.VMEM((TILE_COLS, 32), jnp.float32),
            pltpu.VMEM((3, 3 * width, width), jnp.bfloat16),
            pltpu.VMEM((3, 3 * width, width), jnp.bfloat16),
            pltpu.VMEM((field_rows, width), jnp.float32),
            pltpu.VMEM((field_rows, 3 * width), jnp.bfloat16),
            pltpu.VMEM((field_rows, width), jnp.float32),
            pltpu.VMEM((2, 2, TILE_COLS, width), jnp.bfloat16),
            pltpu.VMEM((2, 2, TILE_ROWS, width), jnp.float32),
            pltpu.VMEM((2, 2, 8, width), jnp.float32),
            pltpu.VMEM((2, 2, TILE_COLS, width), jnp.bfloat16),
            pltpu.VMEM((2, 2, TILE_ROWS, width), jnp.float32),
            pltpu.VMEM((2, 2, 8, width), jnp.float32),
            dma((4,)), dma((shards,)), dma((shards,)), dma((shards,)), dma((shards,)),
            dma((8,)), dma((8,)),
        ],
        compiler_params=pltpu.CompilerParams(
            collective_id=0, has_side_effects=True, vmem_limit_bytes=48 * 1024 * 1024),
        name="exchange",
    )(rows, cells, first_weight, first_bias.reshape(1, -1), second_weight,
      conv_first.reshape(3, 3 * width, width), conv_bias.reshape(1, -1), conv_second.reshape(3, 3 * width, width))


def body(
    observations,
    destinations,
    cells,
    first_weight,
    first_bias,
    second_weight,
    conv_first,
    conv_bias,
    conv_second,
):
    bands = lax.axis_size("lat")
    sectors = lax.axis_size("lon")
    shards = bands * sectors
    capacity = 2 * observations.shape[0] // shards
    rows, spots = dispatch(observations, destinations, cells, shards, capacity)
    return exchange(rows, spots, first_weight, first_bias, second_weight, conv_first, conv_bias, conv_second,
                    bands, (4, 4, 2))


def solution(mesh):
    in_specs = (
        P(("lat", "lon"), None),
        P(("lat", "lon"), None),
        P(("lat", "lon")),
        P(),
        P(),
        P(),
        P(),
        P(),
        P(),
    )
    out_specs = P("lat", "lon", None)
    return jax.shard_map(body, mesh=mesh, in_specs=in_specs, out_specs=out_specs, check_vma=False)
```

```python
import functools

import jax
import jax.numpy as jnp
from jax import lax
from jax.experimental import pallas as pl
from jax.experimental.pallas import tpu as pltpu
from jax.sharding import PartitionSpec as P

TILE_ROWS = 24
TILE_COLS = 48
BLOCK = 256
ROOM = 16384


PITCH = 64


def encode_tile(sums, scale, first_kernel, second_kernel, bias_ref, out_ref, field, shifted, middle,
                row_edges, column_edges, corner_edges, row_halos, column_halos, corner_halos,
                send_halo, recv_halo):
    f32, bf16, i32 = jnp.float32, jnp.bfloat16, jnp.int32
    mesh_id = pl.DeviceIdType.MESH
    bands, sectors = lax.axis_size("lat"), lax.axis_size("lon")
    band, sector = lax.axis_index("lat"), lax.axis_index("lon")
    width = sums.shape[1]

    def at(line, column):
        return (line + 3) * PITCH + column

    for line in range(TILE_ROWS):
        block = sums[pl.ds(line * TILE_COLS, TILE_COLS), :] * scale[:, line:line + 1]
        block = block.astype(bf16)
        field[pl.ds(at(line, 0), TILE_COLS), :] = block.astype(f32)
        if line < 2:
            row_edges[0, line] = block
        if line >= TILE_ROWS - 2:
            row_edges[1, TILE_ROWS - 1 - line] = block
    for side, columns in enumerate(((0, 1), (TILE_COLS - 1, TILE_COLS - 2))):
        for depth, column in enumerate(columns):
            for line in range(TILE_ROWS):
                column_edges[side, depth, pl.ds(line, 1), :] = field[pl.ds(at(line, column), 1), :]
        for end, lines in enumerate(((0, 1), (TILE_ROWS - 1, TILE_ROWS - 2))):
            for i, line in enumerate(lines):
                for j, column in enumerate(columns):
                    corner_edges[end, side, pl.ds(2 * i + j, 1), :] = field[pl.ds(at(line, column), 1), :]

    north = band > 0
    south = band < bands - 1
    vertical = (
        (jnp.where(north, band - 1, 0), jnp.where(north, 0, sectors // 2), jnp.where(north, 1, 0)),
        (jnp.where(south, band + 1, bands - 1), jnp.where(south, 0, sectors // 2), jnp.where(south, 0, 1)),
    )
    copies = []

    def ship(source, target, slot, target_band, shift):
        copies.append(
            pltpu.make_async_remote_copy(
                src_ref=source, dst_ref=target, send_sem=send_halo.at[len(copies)], recv_sem=recv_halo.at[slot],
                device_id=(target_band, lax.rem(sector + shift + 2 * sectors, sectors)), device_id_type=mesh_id))
        copies[-1].start()

    for end, (target_band, shift, landing) in enumerate(vertical):
        ship(row_edges.at[end], row_halos.at[landing], landing, target_band, shift)
    for side, step in enumerate((-1, 1)):
        ship(column_edges.at[side], column_halos.at[1 - side], 2 + 1 - side, band, step)
    for end, (target_band, shift, landing) in enumerate(vertical):
        for side, step in enumerate((-1, 1)):
            ship(corner_edges.at[end, side], corner_halos.at[landing, 1 - side], 4 + 2 * landing + 1 - side,
                 target_band, shift + step)
    arrivals = [row_halos.at[0], row_halos.at[1], column_halos.at[0], column_halos.at[1]]
    arrivals += [corner_halos.at[end, side] for end in range(2) for side in range(2)]
    for slot, buffer in enumerate(arrivals):
        pltpu.make_async_remote_copy(
            src_ref=buffer, dst_ref=buffer, send_sem=send_halo.at[slot], recv_sem=recv_halo.at[slot],
            device_id=(band, sector), device_id_type=mesh_id).wait_recv()

    for end, lines in enumerate(((-1, -2), (TILE_ROWS, TILE_ROWS + 1))):
        for depth, line in enumerate(lines):
            field[pl.ds(at(line, 0), TILE_COLS), :] = row_halos[end, depth].astype(f32)
    for side, columns in enumerate(((-1, -2), (TILE_COLS, TILE_COLS + 1))):
        for depth, column in enumerate(columns):
            for line in range(TILE_ROWS):
                field[pl.ds(at(line, column), 1), :] = column_halos[side, depth, pl.ds(line, 1), :]
        for end, lines in enumerate(((-1, -2), (TILE_ROWS, TILE_ROWS + 1))):
            for i, line in enumerate(lines):
                for j, column in enumerate(columns):
                    field[pl.ds(at(line, column), 1), :] = corner_halos[end, side, pl.ds(2 * i + j, 1), :]

    def spread(array, start, stop):
        for tap in range(3):
            shifted[pl.ds(start, stop - start), tap * width:(tap + 1) * width] = (
                array[pl.ds(start + tap - 1, stop - start), :].astype(bf16))

    low, high = at(-1, -16), at(TILE_ROWS, PITCH)
    spread(field, low - PITCH, high + PITCH)
    total = 0.0
    for tap in range(3):
        total += jnp.dot(shifted[pl.ds(low + (tap - 1) * PITCH, high - low), :], first_kernel[tap],
                         preferred_element_type=f32)
    tall = PITCH + 16
    turned = 0.0
    for tap in range(3):
        lines = jnp.concatenate(
            [shifted[pl.ds(at(line - (tap - 1), -16), tall), :] for line in (-1, TILE_ROWS)], axis=0)
        turned += jnp.dot(lines, first_kernel[tap], preferred_element_type=f32)
    half_bias = 0.5 * bias_ref[...]

    def activate(value):
        half = 0.5 * value + half_bias
        return half + half * jnp.tanh(half)

    middle[pl.ds(low, high - low), :] = activate(total)
    turned = activate(turned)
    spot = lax.broadcasted_iota(i32, (tall, width), 0)
    inside = (spot >= 15) & (spot < 16 + TILE_COLS + 1)
    for index, (line, polar) in enumerate(((-1, band == 0), (TILE_ROWS, band == bands - 1))):
        place = pl.ds(at(line, -16), tall)
        chosen = jnp.where(polar, 1, 0)
        middle[place, :] = jnp.where(
            inside & (chosen == 1), turned[index * tall:(index + 1) * tall], middle[place, :])

    start, stop = at(0, 0), at(TILE_ROWS, 0)
    spread(middle, start - PITCH, stop + PITCH)
    total = field[pl.ds(start, stop - start), :]
    for tap in range(3):
        total += jnp.dot(shifted[pl.ds(start + (tap - 1) * PITCH, stop - start), :], second_kernel[tap],
                         preferred_element_type=f32)
    out_ref[...] = total.reshape(TILE_ROWS, PITCH, width)[:, :TILE_COLS].astype(bf16)
    for copy in copies:
        copy.wait_send()


def partner(step):
    core = lax.rem(step, 2)
    along = lax.rem(lax.div(step, 2), 4)
    half = lax.rem(lax.div(step, 8), 2)
    turn = lax.rem(lax.div(step, 16), 4)
    last = lax.div(step, 64)
    sector = lax.axis_index("lon")
    own_x, own_y, own_core = lax.div(sector, 8), lax.rem(lax.div(sector, 2), 4), lax.rem(sector, 2)
    to_x = lax.rem(own_x + along, 4)
    to_y = lax.rem(own_y + along + turn, 4)
    to_core = lax.rem(own_core + core, 2)
    to_band = lax.rem(lax.axis_index("lat") + along + 2 * half + last, 4)
    return to_band, to_x * 8 + to_y * 2 + to_core


def order_rows(shards, capacity, dest, cell, obs, waits, greet, source, ordered, spots, table, order, order_smem,
               begins, begins_smem, copy_sem):
    values, count_rows = obs.shape
    packing = 128 // values
    f32, bf16, i32 = jnp.float32, jnp.bfloat16, jnp.int32
    lines = count_rows // 128
    span = 4 * BLOCK

    band, sector = partner(lax.broadcasted_iota(i32, (shards, 1), 0))
    owner = band * lax.axis_size("lon") + sector
    lane = lax.broadcasted_iota(i32, (BLOCK, BLOCK + 128), 1)
    row = lax.broadcasted_iota(i32, (BLOCK, BLOCK + 128), 0)
    earlier = jnp.where((row < lane) | (lane >= BLOCK), 1.0, 0.0).astype(bf16)
    value_lane = lax.broadcasted_iota(i32, (values, 128), 1)
    value_row = lax.broadcasted_iota(i32, (values, 128), 0)
    spread = jnp.where(lax.rem(value_lane, values) == value_row, 1.0, 0.0).astype(bf16)
    ranks = lax.broadcasted_iota(i32, (capacity, BLOCK), 0).astype(f32)
    high_lines = lax.broadcasted_iota(i32, (lines, BLOCK), 0)
    low_lines = lax.broadcasted_iota(i32, (128, BLOCK), 0)
    number_lane = lax.broadcasted_iota(i32, (1, BLOCK), 1).astype(f32)

    table[...] = jnp.zeros_like(table)
    order[...] = jnp.zeros_like(order)
    ordered[pl.ds(count_rows, capacity), :] = jnp.zeros((capacity, 128), f32)
    waits[0].wait()

    def count(step, total):
        at = pl.multiple_of(step * (count_rows // 32), count_rows // 32)
        for part in range(count_rows // 32 // 128):
            total += jnp.where(owner == dest[:, pl.ds(at + 128 * part, 128)], 1.0, 0.0)
        for part in range(shards // 32):
            greet(step * (shards // 32) + part)
        return total

    total = lax.fori_loop(0, 32, count, jnp.zeros((shards, 128), f32))
    below = lax.broadcasted_iota(i32, (shards, shards), 0) > lax.broadcasted_iota(i32, (shards, shards), 1)
    begin = jnp.dot(jnp.where(below, 1.0, 0.0).astype(bf16), total.astype(bf16), preferred_element_type=f32)
    begin = jnp.sum(begin, axis=1, keepdims=True)
    begins[...] = jnp.broadcast_to(jnp.clip(begin.astype(i32), 0, count_rows), begins.shape)
    begins_copy = pltpu.make_async_copy(begins, begins_smem, copy_sem.at[0])
    begins_copy.start()
    waits[1].wait()
    waits[2].wait()

    def place(step, carry):
        weights, ranked, highs, lows = [], [], [], []
        for part in range(span // BLOCK):
            at = pl.multiple_of(step * span + part * BLOCK, BLOCK)
            named = jnp.where(owner == dest[:, pl.ds(at, BLOCK)], 1.0, 0.0)
            counted = jnp.dot(named.astype(bf16), earlier, preferred_element_type=f32)
            before = counted[:, :BLOCK] + jnp.concatenate([carry] * (BLOCK // 128), axis=1)
            carry = carry + counted[:, BLOCK:]
            rank = jnp.sum(named * before, axis=0, keepdims=True)
            spot = (rank + jnp.sum(named * begin, axis=0, keepdims=True)).astype(i32)
            cells = cell[:, pl.ds(at, BLOCK)]
            high = lax.shift_right_logical(cells, 6)
            low = cells - lax.shift_left(high, 6)
            weights.append(jnp.concatenate(
                [named * (high + 1).astype(f32), named * low.astype(f32)], axis=0).astype(bf16))
            ranked.append(jnp.where(ranks == rank, 1.0, 0.0).astype(bf16))
            spot_high = lax.shift_right_logical(spot, 7)
            spot_low = spot - lax.shift_left(spot_high, 7)
            here = high_lines == spot_high
            block_number = (step * (span // BLOCK) + part).astype(f32)
            highs.append(jnp.concatenate(
                [jnp.where(here, block_number, 0.0), jnp.where(here, number_lane, 0.0)], axis=0).astype(bf16))
            lows.append(jnp.where(low_lines == spot_low, 1.0, 0.0).astype(bf16))
            source[pl.ds(at, BLOCK), :] = lax.dot_general(
                obs[:, pl.ds(at, BLOCK)].astype(bf16), spread, (((0,), (0,)), ((), ())), preferred_element_type=f32)
        along = (((1,), (1,)), ((), ()))
        table[...] += lax.dot_general(
            jnp.concatenate(weights, axis=1), jnp.concatenate(ranked, axis=1), along, preferred_element_type=f32)
        order[...] += lax.dot_general(
            jnp.concatenate(highs, axis=1), jnp.concatenate(lows, axis=1), along, preferred_element_type=f32)
        return carry

    lax.fori_loop(0, count_rows // span, place, jnp.zeros((shards, 128), f32))

    numbers = order[:lines, :].astype(i32) * BLOCK + order[lines:, :].astype(i32)
    begins_copy.wait()
    begins[pl.ds(0, lines), :] = jnp.clip(numbers, 0, count_rows - 1)
    order_copy = pltpu.make_async_copy(begins.at[pl.ds(0, lines)], order_smem, copy_sem.at[1])
    order_copy.start()
    found = table[:shards, :].astype(i32) * 64 + table[shards:, :].astype(i32) - 64
    found = jnp.where(found >= 0, found, -1)
    absent = jnp.full((shards, 64), -1, i32)
    straight = jnp.concatenate([found, absent], axis=1)
    turned = jnp.concatenate([absent, found], axis=1)
    odd = lax.rem(lax.broadcasted_iota(i32, (shards, 1), 0), 2)
    placed = jnp.where(odd == 1, turned, straight)
    spots[:, 0, :] = placed[:, :128]
    spots[:, 1, :] = placed[:, 128:]
    order_copy.wait()


def exchange_kernel(group, chunk, obs_ref, dest_ref, cell_ref, first_ref, bias_ref, second_ref,
                    conv_first_ref, conv_bias_ref, conv_second_ref, out_ref,
                    obs, dest, cell, source, ordered, table, order, order_smem, begins, begins_smem,
                    outbox, spots, rows_got, cells_got, features, sums, counts, first_kernel, second_kernel,
                    field, shifted, middle,
                    row_edges, column_edges, corner_edges, row_halos, column_halos, corner_halos, own_sem, copy_sem,
                    send_rows, send_cells, recv_rows, recv_cells, send_halo, recv_halo):
    shards, packed, _ = rows_got.shape
    values = first_ref.shape[0]
    width = second_ref.shape[1]
    packing = 128 // values
    capacity = packing * packed
    count_rows = obs.shape[1]
    tile_cells = TILE_ROWS * TILE_COLS
    f32, bf16, i32 = jnp.float32, jnp.bfloat16, jnp.int32
    mesh_id = pl.DeviceIdType.MESH

    barrier = pltpu.get_barrier_semaphore()
    loads = [
        pltpu.make_async_copy(source_ref, target, own_sem.at[number])
        for number, (source_ref, target) in enumerate((
            (dest_ref, dest), (cell_ref, cell), (obs_ref, obs), (conv_first_ref, first_kernel),
            (conv_second_ref, second_kernel)))
    ]
    for copy in loads:
        copy.start()
    kernels = loads[3:]

    def greet(step):
        @pl.when(step > 0)
        def _():
            pl.semaphore_signal(barrier, inc=1, device_id=partner(step), device_id_type=mesh_id)

    order_rows(shards, capacity, dest, cell, obs, loads[:3], greet, source, ordered, spots, table, order, order_smem,
               begins, begins_smem, copy_sem)
    pl.semaphore_wait(barrier, shards - 1)

    def copies(step):
        target = partner(step)
        return (
            pltpu.make_async_remote_copy(
                src_ref=outbox.at[step], dst_ref=rows_got.at[step], send_sem=send_rows.at[step],
                recv_sem=recv_rows.at[step], device_id=target, device_id_type=mesh_id),
            pltpu.make_async_remote_copy(
                src_ref=spots.at[step], dst_ref=cells_got.at[step], send_sem=send_cells.at[step],
                recv_sem=recv_cells.at[step], device_id=target, device_id_type=mesh_id),
        )

    plane_of = lax.broadcasted_iota(i32, (packed, 128), 1) // values

    def pack(step):
        begin = begins_smem[step, 0] & (ROOM - 1)
        rows = ordered[pl.ds(begin, packed), :]
        for plane in range(1, packing):
            rows = jnp.where(plane_of == plane, ordered[pl.ds(begin + plane * packed, packed), :], rows)
        return rows.astype(bf16)

    def send(step):
        outbox[step] = pack(step)
        for copy in copies(step):
            copy.start()

    pair = 2 * capacity

    def gather(turn, _):
        at = pl.multiple_of(turn * pair, pair)
        for line in range(pair // 128):
            for lane in range(128):
                number = order_smem[turn * (pair // 128) + line, lane] & (ROOM - 1)
                ordered[pl.ds(at + line * 128 + lane, 1), :] = source[pl.ds(number, 1), :]

        @pl.when(turn == 0)
        def _():
            rows_got[0] = pack(0)
            cells_got[0] = spots[0]

        @pl.when(turn > 0)
        def _():
            send(2 * turn)

        send(2 * turn + 1)
        return 0

    lax.fori_loop(0, count_rows // pair, gather, 0)

    def send_rest(step, _):
        send(step)
        return 0

    lax.fori_loop(2 * (count_rows // pair), shards, send_rest, 0)

    sums[...] = jnp.zeros_like(sums)
    counts[...] = jnp.zeros_like(counts)
    first = first_ref[...]
    first_high = first.astype(bf16)
    first_low = (first - first_high.astype(f32)).astype(bf16)
    blank = jnp.zeros((values, width), bf16)
    weights = []
    for plane in range(packing):
        pieces = [blank] * (2 * packing)
        pieces[plane] = first_high
        pieces[packing + plane] = first_low
        weights.append(jnp.concatenate(pieces, axis=0))
    half_bias = 0.5 * bias_ref[...]
    lane = lax.broadcasted_iota(i32, (1, 128), 1)

    def receive(step, _):
        for copy in copies(step):
            copy.wait_recv()
        return 0

    def work(number, _):
        base = number * group
        lax.fori_loop(jnp.maximum(base, 1), base + group, receive, 0)
        rows = rows_got[pl.ds(base, group)].reshape(group * packed, 128)
        rows = jnp.concatenate([rows, rows], axis=1)
        for plane in range(packing):
            half = 0.5 * jnp.dot(rows, weights[plane], preferred_element_type=f32) + half_bias
            hidden = (half + half * jnp.tanh(half)).astype(bf16)
            made = jnp.dot(hidden, second_ref[...], preferred_element_type=f32).astype(bf16)
            features[:, plane] = made.reshape(group, packed, width)
        for part in range(group // chunk):
            pieces = []
            for pair in range(part * chunk // 2, (part + 1) * chunk // 2):
                even = cells_got[base + 2 * pair]
                odd = cells_got[base + 2 * pair + 1]
                pieces += [even[0:1], jnp.where(lane < 64, even[1:2], odd[0:1]), odd[1:2]]
            cell = jnp.concatenate(pieces, axis=1)
            span = chunk * capacity
            spots = lax.broadcasted_iota(jnp.int16, (tile_cells, span), 0)
            onehot = jnp.where(spots == cell.astype(jnp.int16), 1.0, 0.0).astype(bf16)
            sums[...] += jnp.dot(
                onehot, features[pl.ds(part * chunk, chunk)].reshape(span, width), preferred_element_type=f32)
            line = lax.shift_right_arithmetic(cell * 1366, 16)
            column = cell - line * TILE_COLS
            lines = jnp.where(lax.broadcasted_iota(i32, (32, span), 0) == line, 1.0, 0.0).astype(bf16)
            columns = jnp.where(
                (lax.broadcasted_iota(i32, (TILE_COLS, span), 0) == column) & (cell >= 0), 1.0, 0.0).astype(bf16)
            counts[...] += lax.dot_general(columns, lines, (((1,), (1,)), ((), ())), preferred_element_type=f32)
        return 0

    lax.fori_loop(0, shards // group, work, 0)

    scale = 1.0 / jnp.maximum(counts[...], 1.0)
    for copy in kernels:
        copy.wait()
    encode_tile(sums, scale, first_kernel, second_kernel, conv_bias_ref, out_ref, field, shifted, middle,
                row_edges, column_edges, corner_edges, row_halos, column_halos, corner_halos, send_halo, recv_halo)

    def drain(step, _):
        for copy in copies(step):
            copy.wait_send()
        return 0

    lax.fori_loop(1, shards, drain, 0)


def exchange(observations, destinations, cells, first_weight, first_bias, second_weight, conv_first, conv_bias,
             conv_second, shards, capacity, group=16, chunk=4):
    count_rows, values = observations.shape
    width = second_weight.shape[1]
    vmem = pl.BlockSpec(memory_space=pltpu.VMEM)
    anywhere = pl.BlockSpec(memory_space=pl.ANY)
    packing = 128 // values
    packed = capacity // packing
    lines = count_rows // 128
    field_rows = (TILE_ROWS + 5) * PITCH + 16
    dma = pltpu.SemaphoreType.DMA
    f32, bf16, i32 = jnp.float32, jnp.bfloat16, jnp.int32
    return pl.pallas_call(
        functools.partial(exchange_kernel, group, chunk),
        out_shape=jax.ShapeDtypeStruct((TILE_ROWS, TILE_COLS, width), bf16),
        in_specs=[anywhere, anywhere, anywhere, vmem, vmem, vmem, anywhere, vmem, anywhere],
        out_specs=vmem,
        scratch_shapes=[
            pltpu.VMEM((values, count_rows), f32),
            pltpu.VMEM((1, count_rows), i32),
            pltpu.VMEM((1, count_rows), i32),
            pltpu.VMEM((ROOM, 128), f32),
            pltpu.VMEM((ROOM + capacity, 128), f32),
            pltpu.VMEM((2 * shards, capacity), f32),
            pltpu.VMEM((2 * lines, 128), f32),
            pltpu.SMEM((lines, 128), i32),
            pltpu.VMEM((shards, 128), i32),
            pltpu.SMEM((shards, 128), i32),
            pltpu.VMEM((shards, packed, 128), bf16),
            pltpu.VMEM((shards, 2, 128), i32),
            pltpu.VMEM((shards, packed, 128), bf16),
            pltpu.VMEM((shards, 2, 128), i32),
            pltpu.VMEM((group, packing, packed, width), bf16),
            pltpu.VMEM((TILE_ROWS * TILE_COLS, width), f32),
            pltpu.VMEM((TILE_COLS, 32), f32),
            pltpu.VMEM((3, 3 * width, width), bf16),
            pltpu.VMEM((3, 3 * width, width), bf16),
            pltpu.VMEM((field_rows, width), f32),
            pltpu.VMEM((field_rows, 3 * width), bf16),
            pltpu.VMEM((field_rows, width), f32),
            pltpu.VMEM((2, 2, TILE_COLS, width), bf16),
            pltpu.VMEM((2, 2, TILE_ROWS, width), f32),
            pltpu.VMEM((2, 2, 8, width), f32),
            pltpu.VMEM((2, 2, TILE_COLS, width), bf16),
            pltpu.VMEM((2, 2, TILE_ROWS, width), f32),
            pltpu.VMEM((2, 2, 8, width), f32),
            dma((5,)), dma((2,)), dma((shards,)), dma((shards,)), dma((shards,)), dma((shards,)),
            dma((8,)), dma((8,)),
        ],
        compiler_params=pltpu.CompilerParams(
            collective_id=0, has_side_effects=True, vmem_limit_bytes=56 * 1024 * 1024),
        name="exchange",
    )(observations.T, destinations.reshape(1, -1), cells.reshape(1, -1), first_weight, first_bias.reshape(1, -1),
      second_weight, conv_first.reshape(3, 3 * width, width), conv_bias.reshape(1, -1),
      conv_second.reshape(3, 3 * width, width))


def body(
    observations,
    destinations,
    cells,
    first_weight,
    first_bias,
    second_weight,
    conv_first,
    conv_bias,
    conv_second,
):
    shards = lax.axis_size("lat") * lax.axis_size("lon")
    capacity = 2 * observations.shape[0] // shards
    return exchange(observations, destinations, cells, first_weight, first_bias, second_weight, conv_first, conv_bias,
                    conv_second, shards, capacity)


def solution(mesh):
    in_specs = (
        P(("lat", "lon"), None),
        P(("lat", "lon"), None),
        P(("lat", "lon")),
        P(),
        P(),
        P(),
        P(),
        P(),
        P(),
    )
    out_specs = P("lat", "lon", None)
    return jax.shard_map(body, mesh=mesh, in_specs=in_specs, out_specs=out_specs, check_vma=False)
```

```python
import functools

import jax
import jax.numpy as jnp
from jax import lax
from jax.experimental import pallas as pl
from jax.experimental.pallas import tpu as pltpu
from jax.sharding import PartitionSpec as P

TILE_ROWS = 24
TILE_COLS = 48
BLOCK = 256
ROOM = 16384


PITCH = 64


def encode_tile(sums, scale, first_kernel, second_kernel, bias_ref, out_ref, field, shifted, middle,
                row_edges, column_edges, corner_edges, row_halos, column_halos, corner_halos,
                send_halo, recv_halo):
    f32, bf16, i32 = jnp.float32, jnp.bfloat16, jnp.int32
    mesh_id = pl.DeviceIdType.MESH
    bands, sectors = lax.axis_size("lat"), lax.axis_size("lon")
    band, sector = lax.axis_index("lat"), lax.axis_index("lon")
    width = sums.shape[1]

    def at(line, column):
        return (line + 3) * PITCH + column

    for line in range(TILE_ROWS):
        block = sums[pl.ds(line * TILE_COLS, TILE_COLS), :] * scale[:, line:line + 1]
        block = block.astype(bf16)
        field[pl.ds(at(line, 0), TILE_COLS), :] = block.astype(f32)
        if line < 2:
            row_edges[0, line] = block
        if line >= TILE_ROWS - 2:
            row_edges[1, TILE_ROWS - 1 - line] = block
    for side, columns in enumerate(((0, 1), (TILE_COLS - 1, TILE_COLS - 2))):
        for depth, column in enumerate(columns):
            for line in range(TILE_ROWS):
                column_edges[side, depth, pl.ds(line, 1), :] = field[pl.ds(at(line, column), 1), :]
        for end, lines in enumerate(((0, 1), (TILE_ROWS - 1, TILE_ROWS - 2))):
            for i, line in enumerate(lines):
                for j, column in enumerate(columns):
                    corner_edges[end, side, pl.ds(2 * i + j, 1), :] = field[pl.ds(at(line, column), 1), :]

    north = band > 0
    south = band < bands - 1
    vertical = (
        (jnp.where(north, band - 1, 0), jnp.where(north, 0, sectors // 2), jnp.where(north, 1, 0)),
        (jnp.where(south, band + 1, bands - 1), jnp.where(south, 0, sectors // 2), jnp.where(south, 0, 1)),
    )
    copies = []

    def ship(source, target, slot, target_band, shift):
        copies.append(
            pltpu.make_async_remote_copy(
                src_ref=source, dst_ref=target, send_sem=send_halo.at[len(copies)], recv_sem=recv_halo.at[slot],
                device_id=(target_band, lax.rem(sector + shift + 2 * sectors, sectors)), device_id_type=mesh_id))
        copies[-1].start()

    for end, (target_band, shift, landing) in enumerate(vertical):
        ship(row_edges.at[end], row_halos.at[landing], landing, target_band, shift)
    for side, step in enumerate((-1, 1)):
        ship(column_edges.at[side], column_halos.at[1 - side], 2 + 1 - side, band, step)
    for end, (target_band, shift, landing) in enumerate(vertical):
        for side, step in enumerate((-1, 1)):
            ship(corner_edges.at[end, side], corner_halos.at[landing, 1 - side], 4 + 2 * landing + 1 - side,
                 target_band, shift + step)
    arrivals = [row_halos.at[0], row_halos.at[1], column_halos.at[0], column_halos.at[1]]
    arrivals += [corner_halos.at[end, side] for end in range(2) for side in range(2)]
    for slot, buffer in enumerate(arrivals):
        pltpu.make_async_remote_copy(
            src_ref=buffer, dst_ref=buffer, send_sem=send_halo.at[slot], recv_sem=recv_halo.at[slot],
            device_id=(band, sector), device_id_type=mesh_id).wait_recv()

    for end, lines in enumerate(((-1, -2), (TILE_ROWS, TILE_ROWS + 1))):
        for depth, line in enumerate(lines):
            field[pl.ds(at(line, 0), TILE_COLS), :] = row_halos[end, depth].astype(f32)
    for side, columns in enumerate(((-1, -2), (TILE_COLS, TILE_COLS + 1))):
        for depth, column in enumerate(columns):
            for line in range(TILE_ROWS):
                field[pl.ds(at(line, column), 1), :] = column_halos[side, depth, pl.ds(line, 1), :]
        for end, lines in enumerate(((-1, -2), (TILE_ROWS, TILE_ROWS + 1))):
            for i, line in enumerate(lines):
                for j, column in enumerate(columns):
                    field[pl.ds(at(line, column), 1), :] = corner_halos[end, side, pl.ds(2 * i + j, 1), :]

    def spread(array, start, stop):
        for tap in range(3):
            shifted[pl.ds(start, stop - start), tap * width:(tap + 1) * width] = (
                array[pl.ds(start + tap - 1, stop - start), :].astype(bf16))

    low, high = at(-1, -16), at(TILE_ROWS, PITCH)
    spread(field, low - PITCH, high + PITCH)
    total = 0.0
    for tap in range(3):
        total += jnp.dot(shifted[pl.ds(low + (tap - 1) * PITCH, high - low), :], first_kernel[tap],
                         preferred_element_type=f32)
    tall = PITCH + 16
    turned = 0.0
    for tap in range(3):
        lines = jnp.concatenate(
            [shifted[pl.ds(at(line - (tap - 1), -16), tall), :] for line in (-1, TILE_ROWS)], axis=0)
        turned += jnp.dot(lines, first_kernel[tap], preferred_element_type=f32)
    half_bias = 0.5 * bias_ref[...]

    def activate(value):
        half = 0.5 * value + half_bias
        return half + half * jnp.tanh(half)

    middle[pl.ds(low, high - low), :] = activate(total)
    turned = activate(turned)
    spot = lax.broadcasted_iota(i32, (tall, width), 0)
    inside = (spot >= 15) & (spot < 16 + TILE_COLS + 1)
    for index, (line, polar) in enumerate(((-1, band == 0), (TILE_ROWS, band == bands - 1))):
        place = pl.ds(at(line, -16), tall)
        chosen = jnp.where(polar, 1, 0)
        middle[place, :] = jnp.where(
            inside & (chosen == 1), turned[index * tall:(index + 1) * tall], middle[place, :])

    start, stop = at(0, 0), at(TILE_ROWS, 0)
    spread(middle, start - PITCH, stop + PITCH)
    total = field[pl.ds(start, stop - start), :]
    for tap in range(3):
        total += jnp.dot(shifted[pl.ds(start + (tap - 1) * PITCH, stop - start), :], second_kernel[tap],
                         preferred_element_type=f32)
    out_ref[...] = total.reshape(TILE_ROWS, PITCH, width)[:, :TILE_COLS].astype(bf16)
    for copy in copies:
        copy.wait_send()


def partner(step):
    core = lax.rem(step, 2)
    along = lax.rem(lax.div(step, 2), 4)
    half = lax.rem(lax.div(step, 8), 2)
    turn = lax.rem(lax.div(step, 16), 4)
    last = lax.div(step, 64)
    sector = lax.axis_index("lon")
    own_x, own_y, own_core = lax.div(sector, 8), lax.rem(lax.div(sector, 2), 4), lax.rem(sector, 2)
    to_x = lax.rem(own_x + along, 4)
    to_y = lax.rem(own_y + along + turn, 4)
    to_core = lax.rem(own_core + core, 2)
    to_band = lax.rem(lax.axis_index("lat") + along + 2 * half + last, 4)
    return to_band, to_x * 8 + to_y * 2 + to_core


def order_rows(shards, capacity, dest, cell, obs, waits, greet, source, ordered, spots, table, order, order_smem,
               begins, begins_smem, copy_sem):
    values, count_rows = obs.shape
    packing = 128 // values
    f32, bf16, i32 = jnp.float32, jnp.bfloat16, jnp.int32
    lines = count_rows // 128
    span = 4 * BLOCK

    band, sector = partner(lax.broadcasted_iota(i32, (shards, 1), 0))
    owner = band * lax.axis_size("lon") + sector
    lane = lax.broadcasted_iota(i32, (BLOCK, BLOCK + 128), 1)
    row = lax.broadcasted_iota(i32, (BLOCK, BLOCK + 128), 0)
    earlier = jnp.where((row < lane) | (lane >= BLOCK), 1.0, 0.0).astype(bf16)
    value_lane = lax.broadcasted_iota(i32, (values, 128), 1)
    value_row = lax.broadcasted_iota(i32, (values, 128), 0)
    spread = jnp.where(lax.rem(value_lane, values) == value_row, 1.0, 0.0).astype(bf16)
    ranks = lax.broadcasted_iota(i32, (capacity, BLOCK), 0).astype(f32)
    high_lines = lax.broadcasted_iota(i32, (lines, BLOCK), 0)
    low_lines = lax.broadcasted_iota(i32, (128, BLOCK), 0)
    number_lane = lax.broadcasted_iota(i32, (1, BLOCK), 1).astype(f32)

    table[...] = jnp.zeros_like(table)
    order[...] = jnp.zeros_like(order)
    ordered[pl.ds(count_rows, capacity), :] = jnp.zeros((capacity, 128), f32)
    waits[0].wait()

    def count(step, total):
        at = pl.multiple_of(step * (count_rows // 32), count_rows // 32)
        for part in range(count_rows // 32 // 128):
            total += jnp.where(owner == dest[:, pl.ds(at + 128 * part, 128)], 1.0, 0.0)
        for part in range(shards // 32):
            greet(step * (shards // 32) + part)
        return total

    total = lax.fori_loop(0, 32, count, jnp.zeros((shards, 128), f32))
    below = lax.broadcasted_iota(i32, (shards, shards), 0) > lax.broadcasted_iota(i32, (shards, shards), 1)
    begin = jnp.dot(jnp.where(below, 1.0, 0.0).astype(bf16), total.astype(bf16), preferred_element_type=f32)
    begin = jnp.sum(begin, axis=1, keepdims=True)
    begins[...] = jnp.broadcast_to(jnp.clip(begin.astype(i32), 0, count_rows), begins.shape)
    begins_copy = pltpu.make_async_copy(begins, begins_smem, copy_sem.at[0])
    begins_copy.start()
    waits[1].wait()
    waits[2].wait()

    def place(step, carry):
        weights, ranked, highs, lows = [], [], [], []
        for part in range(span // BLOCK):
            at = pl.multiple_of(step * span + part * BLOCK, BLOCK)
            named = jnp.where(owner == dest[:, pl.ds(at, BLOCK)], 1.0, 0.0)
            counted = jnp.dot(named.astype(bf16), earlier, preferred_element_type=f32)
            before = counted[:, :BLOCK] + jnp.concatenate([carry] * (BLOCK // 128), axis=1)
            carry = carry + counted[:, BLOCK:]
            rank = jnp.sum(named * before, axis=0, keepdims=True)
            spot = (rank + jnp.sum(named * begin, axis=0, keepdims=True)).astype(i32)
            cells = cell[:, pl.ds(at, BLOCK)]
            high = lax.shift_right_logical(cells, 6)
            low = cells - lax.shift_left(high, 6)
            weights.append(jnp.concatenate(
                [named * (high + 1).astype(f32), named * low.astype(f32)], axis=0).astype(bf16))
            ranked.append(jnp.where(ranks == rank, 1.0, 0.0).astype(bf16))
            spot_high = lax.shift_right_logical(spot, 7)
            spot_low = spot - lax.shift_left(spot_high, 7)
            here = high_lines == spot_high
            block_number = (step * (span // BLOCK) + part).astype(f32)
            highs.append(jnp.concatenate(
                [jnp.where(here, block_number, 0.0), jnp.where(here, number_lane, 0.0)], axis=0).astype(bf16))
            lows.append(jnp.where(low_lines == spot_low, 1.0, 0.0).astype(bf16))
            source[pl.ds(at, BLOCK), :] = lax.dot_general(
                obs[:, pl.ds(at, BLOCK)].astype(bf16), spread, (((0,), (0,)), ((), ())), preferred_element_type=f32)
        along = (((1,), (1,)), ((), ()))
        table[...] += lax.dot_general(
            jnp.concatenate(weights, axis=1), jnp.concatenate(ranked, axis=1), along, preferred_element_type=f32)
        order[...] += lax.dot_general(
            jnp.concatenate(highs, axis=1), jnp.concatenate(lows, axis=1), along, preferred_element_type=f32)
        return carry

    lax.fori_loop(0, count_rows // span, place, jnp.zeros((shards, 128), f32))

    numbers = order[:lines, :].astype(i32) * BLOCK + order[lines:, :].astype(i32)
    begins_copy.wait()
    begins[pl.ds(0, lines), :] = jnp.clip(numbers, 0, count_rows - 1)
    order_copy = pltpu.make_async_copy(begins.at[pl.ds(0, lines)], order_smem, copy_sem.at[1])
    order_copy.start()
    found = table[:shards, :].astype(i32) * 64 + table[shards:, :].astype(i32) - 64
    found = jnp.where(found >= 0, found, -1)
    absent = jnp.full((shards, 64), -1, i32)
    straight = jnp.concatenate([found, absent], axis=1)
    turned = jnp.concatenate([absent, found], axis=1)
    odd = lax.rem(lax.broadcasted_iota(i32, (shards, 1), 0), 2)
    placed = jnp.where(odd == 1, turned, straight)
    spots[:, 0, :] = placed[:, :128]
    spots[:, 1, :] = placed[:, 128:]
    order_copy.wait()


def exchange_kernel(group, chunk, obs_ref, dest_ref, cell_ref, first_ref, bias_ref, second_ref,
                    conv_first_ref, conv_bias_ref, conv_second_ref, out_ref,
                    obs, dest, cell, source, ordered, table, order, order_smem, begins, begins_smem,
                    outbox, spots, rows_got, cells_got, features, sums, counts, first_kernel, second_kernel,
                    field, shifted, middle,
                    row_edges, column_edges, corner_edges, row_halos, column_halos, corner_halos, own_sem, copy_sem,
                    send_rows, send_cells, recv_rows, recv_cells, send_halo, recv_halo):
    shards, packed, _ = rows_got.shape
    values = first_ref.shape[0]
    width = second_ref.shape[1]
    packing = 128 // values
    capacity = packing * packed
    count_rows = obs.shape[1]
    tile_cells = TILE_ROWS * TILE_COLS
    f32, bf16, i32 = jnp.float32, jnp.bfloat16, jnp.int32
    mesh_id = pl.DeviceIdType.MESH

    barrier = pltpu.get_barrier_semaphore()
    loads = [
        pltpu.make_async_copy(source_ref, target, own_sem.at[number])
        for number, (source_ref, target) in enumerate((
            (dest_ref, dest), (cell_ref, cell), (obs_ref, obs), (conv_first_ref, first_kernel),
            (conv_second_ref, second_kernel)))
    ]
    for copy in loads:
        copy.start()
    kernels = loads[3:]

    def greet(step):
        @pl.when(step > 0)
        def _():
            pl.semaphore_signal(barrier, inc=1, device_id=partner(step), device_id_type=mesh_id)

    order_rows(shards, capacity, dest, cell, obs, loads[:3], greet, source, ordered, spots, table, order, order_smem,
               begins, begins_smem, copy_sem)
    pl.semaphore_wait(barrier, shards - 1)

    def copies(step):
        target = partner(step)
        return (
            pltpu.make_async_remote_copy(
                src_ref=outbox.at[step], dst_ref=rows_got.at[step], send_sem=send_rows.at[step],
                recv_sem=recv_rows.at[step], device_id=target, device_id_type=mesh_id),
            pltpu.make_async_remote_copy(
                src_ref=spots.at[step], dst_ref=cells_got.at[step], send_sem=send_cells.at[step],
                recv_sem=recv_cells.at[step], device_id=target, device_id_type=mesh_id),
        )

    plane_of = lax.broadcasted_iota(i32, (packed, 128), 1) // values

    def pack(step):
        begin = begins_smem[step, 0] & (ROOM - 1)
        rows = ordered[pl.ds(begin, packed), :]
        for plane in range(1, packing):
            rows = jnp.where(plane_of == plane, ordered[pl.ds(begin + plane * packed, packed), :], rows)
        return rows.astype(bf16)

    def send(step):
        outbox[step] = pack(step)
        for copy in copies(step):
            copy.start()

    pair = 2 * capacity

    def gather(turn, _):
        at = pl.multiple_of(turn * pair, pair)
        for line in range(pair // 128):
            for lane in range(128):
                number = order_smem[turn * (pair // 128) + line, lane]
                ordered[pl.ds(at + line * 128 + lane, 1), :] = source[pl.ds(number, 1), :]

        @pl.when(turn == 0)
        def _():
            rows_got[0] = pack(0)
            cells_got[0] = spots[0]

        @pl.when(turn > 0)
        def _():
            send(2 * turn)

        send(2 * turn + 1)
        return 0

    lax.fori_loop(0, count_rows // pair, gather, 0)

    def send_rest(step, _):
        send(step)
        return 0

    lax.fori_loop(2 * (count_rows // pair), shards, send_rest, 0)

    sums[...] = jnp.zeros_like(sums)
    counts[...] = jnp.zeros_like(counts)
    first = first_ref[...]
    first_high = first.astype(bf16)
    first_low = (first - first_high.astype(f32)).astype(bf16)
    blank = jnp.zeros((values, width), bf16)
    weights = []
    for plane in range(packing):
        pieces = [blank] * (2 * packing)
        pieces[plane] = first_high
        pieces[packing + plane] = first_low
        weights.append(jnp.concatenate(pieces, axis=0))
    half_bias = 0.5 * bias_ref[...]
    lane = lax.broadcasted_iota(i32, (1, 128), 1)

    def receive(step, _):
        for copy in copies(step):
            copy.wait_recv()
        return 0

    def work(number, _):
        base = number * group
        lax.fori_loop(jnp.maximum(base, 1), base + group, receive, 0)
        rows = rows_got[pl.ds(base, group)].reshape(group * packed, 128)
        rows = jnp.concatenate([rows, rows], axis=1)
        for plane in range(packing):
            half = 0.5 * jnp.dot(rows, weights[plane], preferred_element_type=f32) + half_bias
            hidden = (half + half * jnp.tanh(half)).astype(bf16)
            made = jnp.dot(hidden, second_ref[...], preferred_element_type=f32).astype(bf16)
            features[:, plane] = made.reshape(group, packed, width)
        for part in range(group // chunk):
            pieces = []
            for pair in range(part * chunk // 2, (part + 1) * chunk // 2):
                even = cells_got[base + 2 * pair]
                odd = cells_got[base + 2 * pair + 1]
                pieces += [even[0:1], jnp.where(lane < 64, even[1:2], odd[0:1]), odd[1:2]]
            cell = jnp.concatenate(pieces, axis=1)
            span = chunk * capacity
            spots = lax.broadcasted_iota(i32, (tile_cells, span), 0)
            onehot = jnp.where(spots == cell, 1.0, 0.0).astype(bf16)
            sums[...] += jnp.dot(
                onehot, features[pl.ds(part * chunk, chunk)].reshape(span, width), preferred_element_type=f32)
            line = lax.shift_right_arithmetic(cell * 1366, 16)
            column = cell - line * TILE_COLS
            lines = jnp.where(lax.broadcasted_iota(i32, (32, span), 0) == line, 1.0, 0.0).astype(bf16)
            columns = jnp.where(
                (lax.broadcasted_iota(i32, (TILE_COLS, span), 0) == column) & (cell >= 0), 1.0, 0.0).astype(bf16)
            counts[...] += lax.dot_general(columns, lines, (((1,), (1,)), ((), ())), preferred_element_type=f32)
        return 0

    lax.fori_loop(0, shards // group, work, 0)

    scale = 1.0 / jnp.maximum(counts[...], 1.0)
    for copy in kernels:
        copy.wait()
    encode_tile(sums, scale, first_kernel, second_kernel, conv_bias_ref, out_ref, field, shifted, middle,
                row_edges, column_edges, corner_edges, row_halos, column_halos, corner_halos, send_halo, recv_halo)

    def drain(step, _):
        for copy in copies(step):
            copy.wait_send()
        return 0

    lax.fori_loop(1, shards, drain, 0)


def exchange(observations, destinations, cells, first_weight, first_bias, second_weight, conv_first, conv_bias,
             conv_second, shards, capacity, group=16, chunk=4):
    count_rows, values = observations.shape
    width = second_weight.shape[1]
    vmem = pl.BlockSpec(memory_space=pltpu.VMEM)
    anywhere = pl.BlockSpec(memory_space=pl.ANY)
    packing = 128 // values
    packed = capacity // packing
    lines = count_rows // 128
    field_rows = (TILE_ROWS + 5) * PITCH + 16
    dma = pltpu.SemaphoreType.DMA
    f32, bf16, i32 = jnp.float32, jnp.bfloat16, jnp.int32
    return pl.pallas_call(
        functools.partial(exchange_kernel, group, chunk),
        out_shape=jax.ShapeDtypeStruct((TILE_ROWS, TILE_COLS, width), bf16),
        in_specs=[anywhere, anywhere, anywhere, vmem, vmem, vmem, anywhere, vmem, anywhere],
        out_specs=vmem,
        scratch_shapes=[
            pltpu.VMEM((values, count_rows), f32),
            pltpu.VMEM((1, count_rows), i32),
            pltpu.VMEM((1, count_rows), i32),
            pltpu.VMEM((ROOM, 128), f32),
            pltpu.VMEM((ROOM + capacity, 128), f32),
            pltpu.VMEM((2 * shards, capacity), f32),
            pltpu.VMEM((2 * lines, 128), f32),
            pltpu.SMEM((lines, 128), i32),
            pltpu.VMEM((shards, 128), i32),
            pltpu.SMEM((shards, 128), i32),
            pltpu.VMEM((shards, packed, 128), bf16),
            pltpu.VMEM((shards, 2, 128), i32),
            pltpu.VMEM((shards, packed, 128), bf16),
            pltpu.VMEM((shards, 2, 128), i32),
            pltpu.VMEM((group, packing, packed, width), bf16),
            pltpu.VMEM((TILE_ROWS * TILE_COLS, width), f32),
            pltpu.VMEM((TILE_COLS, 32), f32),
            pltpu.VMEM((3, 3 * width, width), bf16),
            pltpu.VMEM((3, 3 * width, width), bf16),
            pltpu.VMEM((field_rows, width), f32),
            pltpu.VMEM((field_rows, 3 * width), bf16),
            pltpu.VMEM((field_rows, width), f32),
            pltpu.VMEM((2, 2, TILE_COLS, width), bf16),
            pltpu.VMEM((2, 2, TILE_ROWS, width), f32),
            pltpu.VMEM((2, 2, 8, width), f32),
            pltpu.VMEM((2, 2, TILE_COLS, width), bf16),
            pltpu.VMEM((2, 2, TILE_ROWS, width), f32),
            pltpu.VMEM((2, 2, 8, width), f32),
            dma((5,)), dma((2,)), dma((shards,)), dma((shards,)), dma((shards,)), dma((shards,)),
            dma((8,)), dma((8,)),
        ],
        compiler_params=pltpu.CompilerParams(
            collective_id=0, has_side_effects=True, vmem_limit_bytes=56 * 1024 * 1024),
        name="exchange",
    )(observations.T, destinations.reshape(1, -1), cells.reshape(1, -1), first_weight, first_bias.reshape(1, -1),
      second_weight, conv_first.reshape(3, 3 * width, width), conv_bias.reshape(1, -1),
      conv_second.reshape(3, 3 * width, width))


def body(
    observations,
    destinations,
    cells,
    first_weight,
    first_bias,
    second_weight,
    conv_first,
    conv_bias,
    conv_second,
):
    shards = lax.axis_size("lat") * lax.axis_size("lon")
    capacity = 2 * observations.shape[0] // shards
    return exchange(observations, destinations, cells, first_weight, first_bias, second_weight, conv_first, conv_bias,
                    conv_second, shards, capacity)


def solution(mesh):
    in_specs = (
        P(("lat", "lon"), None),
        P(("lat", "lon"), None),
        P(("lat", "lon")),
        P(),
        P(),
        P(),
        P(),
        P(),
        P(),
    )
    out_specs = P("lat", "lon", None)
    return jax.shard_map(body, mesh=mesh, in_specs=in_specs, out_specs=out_specs, check_vma=False)
```

```python
import functools

import jax
import jax.numpy as jnp
from jax import lax
from jax.experimental import pallas as pl
from jax.experimental.pallas import tpu as pltpu
from jax.sharding import PartitionSpec as P

TILE_ROWS = 24
TILE_COLS = 48
BLOCK = 256
ROOM = 16384


PITCH = 64


def encode_tile(sums, scale, first_kernel, second_kernel, bias_ref, out_ref, field, shifted, middle,
                column_stage, row_edges, column_edges, corner_edges, row_halos, column_halos, corner_halos,
                send_halo, recv_halo):
    f32, bf16, i32 = jnp.float32, jnp.bfloat16, jnp.int32
    mesh_id = pl.DeviceIdType.MESH
    bands, sectors = lax.axis_size("lat"), lax.axis_size("lon")
    band, sector = lax.axis_index("lat"), lax.axis_index("lon")
    width = sums.shape[1]

    def at(line, column):
        return (line + 3) * PITCH + column

    north = band > 0
    south = band < bands - 1
    vertical = (
        (jnp.where(north, band - 1, 0), jnp.where(north, 0, sectors // 2), jnp.where(north, 1, 0)),
        (jnp.where(south, band + 1, bands - 1), jnp.where(south, 0, sectors // 2), jnp.where(south, 0, 1)),
    )
    copies = []

    def ship(source, target, slot, target_band, shift):
        copies.append(
            pltpu.make_async_remote_copy(
                src_ref=source, dst_ref=target, send_sem=send_halo.at[len(copies)], recv_sem=recv_halo.at[slot],
                device_id=(target_band, lax.rem(sector + shift + 2 * sectors, sectors)), device_id_type=mesh_id))
        copies[-1].start()

    def average(line):
        block = sums[pl.ds(line * TILE_COLS, TILE_COLS), :] * scale[:, line:line + 1]
        block = block.astype(bf16)
        field[pl.ds(at(line, 0), TILE_COLS), :] = block.astype(f32)
        return block

    ends = ((0, 1), (TILE_ROWS - 1, TILE_ROWS - 2))
    borders = ((0, 1), (TILE_COLS - 1, TILE_COLS - 2))
    for end, (target_band, shift, landing) in enumerate(vertical):
        for depth, line in enumerate(ends[end]):
            row_edges[end, depth] = average(line)
        ship(row_edges.at[end], row_halos.at[landing], landing, target_band, shift)
    for end, (target_band, shift, landing) in enumerate(vertical):
        for side, step in enumerate((-1, 1)):
            for i, line in enumerate(ends[end]):
                for j, column in enumerate(borders[side]):
                    corner_edges[end, side, pl.ds(2 * i + j, 1), :] = field[pl.ds(at(line, column), 1), :]
            ship(corner_edges.at[end, side], corner_halos.at[landing, 1 - side], 4 + 2 * landing + 1 - side,
                 target_band, shift + step)
    for line in range(2, TILE_ROWS - 2):
        average(line)
    blank = jnp.zeros((8, width), f32)
    for side, step in enumerate((-1, 1)):
        for depth, column in enumerate(borders[side]):
            for line in range(TILE_ROWS):
                column_stage[side, depth, pl.ds(line, 1), :] = field[pl.ds(at(line, column), 1), :]
            column_edges[side, depth] = jnp.concatenate([column_stage[side, depth], blank], axis=0).astype(bf16)
        ship(column_edges.at[side], column_halos.at[1 - side], 2 + 1 - side, band, step)
    arrivals = [row_halos.at[0], row_halos.at[1], column_halos.at[0], column_halos.at[1]]
    arrivals += [corner_halos.at[end, side] for end in range(2) for side in range(2)]
    for slot, buffer in enumerate(arrivals):
        pltpu.make_async_remote_copy(
            src_ref=buffer, dst_ref=buffer, send_sem=send_halo.at[slot], recv_sem=recv_halo.at[slot],
            device_id=(band, sector), device_id_type=mesh_id).wait_recv()

    for end, lines in enumerate(((-1, -2), (TILE_ROWS, TILE_ROWS + 1))):
        for depth, line in enumerate(lines):
            field[pl.ds(at(line, 0), TILE_COLS), :] = row_halos[end, depth].astype(f32)
    for side, columns in enumerate(((-1, -2), (TILE_COLS, TILE_COLS + 1))):
        for depth, column in enumerate(columns):
            column_stage[side, depth] = column_halos[side, depth].astype(f32)[:TILE_ROWS]
            for line in range(TILE_ROWS):
                field[pl.ds(at(line, column), 1), :] = column_stage[side, depth, pl.ds(line, 1), :]
        for end, lines in enumerate(((-1, -2), (TILE_ROWS, TILE_ROWS + 1))):
            for i, line in enumerate(lines):
                for j, column in enumerate(columns):
                    field[pl.ds(at(line, column), 1), :] = corner_halos[end, side, pl.ds(2 * i + j, 1), :]

    def spread(array, start, stop):
        for tap in range(3):
            shifted[pl.ds(start, stop - start), tap * width:(tap + 1) * width] = (
                array[pl.ds(start + tap - 1, stop - start), :].astype(bf16))

    low, high = at(-1, -16), at(TILE_ROWS, PITCH)
    spread(field, low - PITCH, high + PITCH)
    parts = [shifted[pl.ds(low + (tap - 1) * PITCH, high - low), :] for tap in range(3)]
    total = jnp.dot(jnp.concatenate(parts, axis=1), first_kernel[...].reshape(9 * width, width),
                    preferred_element_type=f32)
    tall = PITCH + 16
    turned = 0.0
    for tap in range(3):
        lines = jnp.concatenate(
            [shifted[pl.ds(at(line - (tap - 1), -16), tall), :] for line in (-1, TILE_ROWS)], axis=0)
        turned += jnp.dot(lines, first_kernel[tap], preferred_element_type=f32)
    half_bias = 0.5 * bias_ref[...]

    def activate(value):
        half = 0.5 * value + half_bias
        return half + half * jnp.tanh(half)

    middle[pl.ds(low, high - low), :] = activate(total)
    turned = activate(turned)
    spot = lax.broadcasted_iota(i32, (tall, width), 0)
    inside = (spot >= 15) & (spot < 16 + TILE_COLS + 1)
    for index, (line, polar) in enumerate(((-1, band == 0), (TILE_ROWS, band == bands - 1))):
        place = pl.ds(at(line, -16), tall)
        chosen = jnp.where(polar, 1, 0)
        middle[place, :] = jnp.where(
            inside & (chosen == 1), turned[index * tall:(index + 1) * tall], middle[place, :])

    start, stop = at(0, 0), at(TILE_ROWS, 0)
    spread(middle, start - PITCH, stop + PITCH)
    total = field[pl.ds(start, stop - start), :]
    parts = [shifted[pl.ds(start + (tap - 1) * PITCH, stop - start), :] for tap in range(3)]
    total += jnp.dot(jnp.concatenate(parts, axis=1), second_kernel[...].reshape(9 * width, width),
                     preferred_element_type=f32)
    out_ref[...] = total.reshape(TILE_ROWS, PITCH, width)[:, :TILE_COLS].astype(bf16)
    for copy in copies:
        copy.wait_send()


def partner(step):
    core = lax.rem(step, 2)
    along = lax.rem(lax.div(step, 2), 4)
    half = lax.rem(lax.div(step, 8), 2)
    turn = lax.rem(lax.div(step, 16), 4)
    last = lax.div(step, 64)
    sector = lax.axis_index("lon")
    own_x, own_y, own_core = lax.div(sector, 8), lax.rem(lax.div(sector, 2), 4), lax.rem(sector, 2)
    to_x = lax.rem(own_x + along, 4)
    to_y = lax.rem(own_y + along + turn, 4)
    to_core = lax.rem(own_core + core, 2)
    to_band = lax.rem(lax.axis_index("lat") + along + 2 * half + last, 4)
    return to_band, to_x * 8 + to_y * 2 + to_core


def order_rows(shards, capacity, dest, cell, obs, waits, source, ordered, spots, table, order, order_smem,
               begins, begins_smem, copy_sem):
    values, count_rows = obs.shape
    packing = 128 // values
    f32, bf16, i32 = jnp.float32, jnp.bfloat16, jnp.int32
    lines = count_rows // 128
    span = 4 * BLOCK

    band, sector = partner(lax.broadcasted_iota(i32, (shards, 1), 0))
    owner = band * lax.axis_size("lon") + sector
    lane = lax.broadcasted_iota(i32, (BLOCK, BLOCK + 128), 1)
    row = lax.broadcasted_iota(i32, (BLOCK, BLOCK + 128), 0)
    earlier = jnp.where((row < lane) | (lane >= BLOCK), 1.0, 0.0).astype(bf16)
    value_lane = lax.broadcasted_iota(i32, (values, 128), 1)
    value_row = lax.broadcasted_iota(i32, (values, 128), 0)
    spread = jnp.where(lax.rem(value_lane, values) == value_row, 1.0, 0.0).astype(bf16)
    ranks = lax.broadcasted_iota(i32, (capacity, BLOCK), 0).astype(f32)
    high_lines = lax.broadcasted_iota(i32, (lines, BLOCK), 0)
    low_lines = lax.broadcasted_iota(i32, (128, BLOCK), 0)
    number_lane = lax.broadcasted_iota(i32, (1, BLOCK), 1).astype(f32)

    table[...] = jnp.zeros_like(table)
    order[...] = jnp.zeros_like(order)
    ordered[pl.ds(count_rows, capacity), :] = jnp.zeros((capacity, 128), f32)
    waits[0].wait()

    def count(step, total):
        at = pl.multiple_of(step * (count_rows // 32), count_rows // 32)
        for part in range(count_rows // 32 // 128):
            total += jnp.where(owner == dest[:, pl.ds(at + 128 * part, 128)], 1.0, 0.0)
        return total

    total = lax.fori_loop(0, 32, count, jnp.zeros((shards, 128), f32))
    below = lax.broadcasted_iota(i32, (shards, shards), 0) > lax.broadcasted_iota(i32, (shards, shards), 1)
    begin = jnp.dot(jnp.where(below, 1.0, 0.0).astype(bf16), total.astype(bf16), preferred_element_type=f32)
    begin = jnp.sum(begin, axis=1, keepdims=True)
    begins[...] = jnp.broadcast_to(jnp.clip(begin.astype(i32), 0, count_rows), begins.shape)
    begins_copy = pltpu.make_async_copy(begins, begins_smem, copy_sem.at[0])
    begins_copy.start()
    waits[1].wait()
    waits[2].wait()

    def place(step, carry):
        weights, ranked, highs, lows = [], [], [], []
        for part in range(span // BLOCK):
            at = pl.multiple_of(step * span + part * BLOCK, BLOCK)
            named = jnp.where(owner == dest[:, pl.ds(at, BLOCK)], 1.0, 0.0)
            counted = jnp.dot(named.astype(bf16), earlier, preferred_element_type=f32)
            before = counted[:, :BLOCK] + jnp.concatenate([carry] * (BLOCK // 128), axis=1)
            carry = carry + counted[:, BLOCK:]
            rank = jnp.sum(named * before, axis=0, keepdims=True)
            spot = (rank + jnp.sum(named * begin, axis=0, keepdims=True)).astype(i32)
            cells = cell[:, pl.ds(at, BLOCK)]
            high = lax.shift_right_logical(cells, 6)
            low = cells - lax.shift_left(high, 6)
            weights.append(jnp.concatenate(
                [named * (high + 1).astype(f32), named * low.astype(f32)], axis=0).astype(bf16))
            ranked.append(jnp.where(ranks == rank, 1.0, 0.0).astype(bf16))
            spot_high = lax.shift_right_logical(spot, 7)
            spot_low = spot - lax.shift_left(spot_high, 7)
            here = high_lines == spot_high
            block_number = (step * (span // BLOCK) + part).astype(f32)
            highs.append(jnp.concatenate(
                [jnp.where(here, block_number, 0.0), jnp.where(here, number_lane, 0.0)], axis=0).astype(bf16))
            lows.append(jnp.where(low_lines == spot_low, 1.0, 0.0).astype(bf16))
            source[pl.ds(at, BLOCK), :] = lax.dot_general(
                obs[:, pl.ds(at, BLOCK)].astype(bf16), spread, (((0,), (0,)), ((), ())), preferred_element_type=f32)
        along = (((1,), (1,)), ((), ()))
        table[...] += lax.dot_general(
            jnp.concatenate(weights, axis=1), jnp.concatenate(ranked, axis=1), along, preferred_element_type=f32)
        order[...] += lax.dot_general(
            jnp.concatenate(highs, axis=1), jnp.concatenate(lows, axis=1), along, preferred_element_type=f32)
        return carry

    lax.fori_loop(0, count_rows // span, place, jnp.zeros((shards, 128), f32), unroll=2)

    numbers = order[:lines, :].astype(i32) * BLOCK + order[lines:, :].astype(i32)
    begins_copy.wait()
    begins[pl.ds(0, lines), :] = jnp.clip(numbers, 0, count_rows - 1)
    order_copy = pltpu.make_async_copy(begins.at[pl.ds(0, lines)], order_smem, copy_sem.at[1])
    order_copy.start()
    found = table[:shards, :].astype(i32) * 64 + table[shards:, :].astype(i32) - 64
    found = jnp.where(found >= 0, found, -1)
    absent = jnp.full((shards, 64), -1, i32)
    straight = jnp.concatenate([found, absent], axis=1)
    turned = jnp.concatenate([absent, found], axis=1)
    odd = lax.rem(lax.broadcasted_iota(i32, (shards, 1), 0), 2)
    placed = jnp.where(odd == 1, turned, straight)
    spots[:, 0, :] = placed[:, :128]
    spots[:, 1, :] = placed[:, 128:]
    order_copy.wait()


def exchange_kernel(group, chunk, obs_ref, dest_ref, cell_ref, first_ref, bias_ref, second_ref,
                    conv_first_ref, conv_bias_ref, conv_second_ref, out_ref,
                    obs, dest, cell, source, ordered, table, order, order_smem, begins, begins_smem,
                    outbox, spots, rows_got, cells_got, features, sums, counts, first_kernel, second_kernel,
                    field, shifted, middle,
                    column_stage, row_edges, column_edges, corner_edges, row_halos, column_halos, corner_halos, own_sem, copy_sem,
                    send_rows, send_cells, recv_rows, recv_cells, send_halo, recv_halo):
    shards, packed, _ = rows_got.shape
    values = first_ref.shape[0]
    width = second_ref.shape[1]
    packing = 128 // values
    capacity = packing * packed
    count_rows = obs.shape[1]
    tile_cells = TILE_ROWS * TILE_COLS
    f32, bf16, i32 = jnp.float32, jnp.bfloat16, jnp.int32
    mesh_id = pl.DeviceIdType.MESH

    barrier = pltpu.get_barrier_semaphore()
    loads = [
        pltpu.make_async_copy(source_ref, target, own_sem.at[number])
        for number, (source_ref, target) in enumerate((
            (dest_ref, dest), (cell_ref, cell), (obs_ref, obs), (conv_first_ref, first_kernel),
            (conv_second_ref, second_kernel)))
    ]
    for copy in loads:
        copy.start()
    kernels = loads[3:]

    band, sector = lax.axis_index("lat"), lax.axis_index("lon")
    bands = [lax.rem(band + shift, 4) for shift in range(4)]
    along_x = [8 * lax.rem(lax.div(sector, 8) + shift, 4) for shift in range(4)]
    along_y = [2 * lax.rem(lax.div(sector, 2) + shift, 4) for shift in range(4)]
    cores = [lax.rem(sector, 2), 1 - lax.rem(sector, 2)]
    for x in along_x:
        for y in along_y:
            for core in cores:
                place = x + y + core
                for to_band in bands:
                    if x is along_x[0] and y is along_y[0] and core is cores[0] and to_band is bands[0]:
                        continue
                    pl.semaphore_signal(barrier, inc=1, device_id=(to_band, place), device_id_type=mesh_id)

    order_rows(shards, capacity, dest, cell, obs, loads[:3], source, ordered, spots, table, order, order_smem,
               begins, begins_smem, copy_sem)
    pl.semaphore_wait(barrier, shards - 1)

    def copies(step):
        target = partner(step)
        return (
            pltpu.make_async_remote_copy(
                src_ref=outbox.at[step], dst_ref=rows_got.at[step], send_sem=send_rows.at[step],
                recv_sem=recv_rows.at[step], device_id=target, device_id_type=mesh_id),
            pltpu.make_async_remote_copy(
                src_ref=spots.at[step], dst_ref=cells_got.at[step], send_sem=send_cells.at[step],
                recv_sem=recv_cells.at[step], device_id=target, device_id_type=mesh_id),
        )

    plane_of = lax.broadcasted_iota(i32, (packed, 128), 1) // values

    def pack(step):
        begin = begins_smem[step, 0] & (ROOM - 1)
        rows = ordered[pl.ds(begin, packed), :]
        for plane in range(1, packing):
            rows = jnp.where(plane_of == plane, ordered[pl.ds(begin + plane * packed, packed), :], rows)
        return rows.astype(bf16)

    def send(step):
        outbox[step] = pack(step)
        for copy in copies(step):
            copy.start()

    pair = 2 * capacity

    def gather(turn, _):
        at = pl.multiple_of(turn * pair, pair)
        for line in range(pair // 128):
            for lane in range(128):
                number = order_smem[turn * (pair // 128) + line, lane]
                ordered[pl.ds(at + line * 128 + lane, 1), :] = source[pl.ds(number, 1), :]

        @pl.when(turn == 0)
        def _():
            rows_got[0] = pack(0)
            cells_got[0] = spots[0]

        @pl.when(turn > 0)
        def _():
            send(2 * turn)

        send(2 * turn + 1)
        return 0

    lax.fori_loop(0, count_rows // pair, gather, 0)

    def send_rest(step, _):
        send(step)
        return 0

    lax.fori_loop(2 * (count_rows // pair), shards, send_rest, 0)

    sums[...] = jnp.zeros_like(sums)
    counts[...] = jnp.zeros_like(counts)
    first = first_ref[...]
    first_high = first.astype(bf16)
    first_low = (first - first_high.astype(f32)).astype(bf16)
    blank = jnp.zeros((values, width), bf16)
    weights = []
    for plane in range(packing):
        pieces = [blank] * (2 * packing)
        pieces[plane] = first_high
        pieces[packing + plane] = first_low
        weights.append(jnp.concatenate(pieces, axis=0))
    half_bias = 0.5 * bias_ref[...]
    lane = lax.broadcasted_iota(i32, (1, 128), 1)

    def receive(step, _):
        for copy in copies(step):
            copy.wait_recv()
        return 0

    def work(number, _):
        base = number * group
        lax.fori_loop(jnp.maximum(base, 1), base + group, receive, 0)
        rows = rows_got[pl.ds(base, group)].reshape(group * packed, 128)
        rows = jnp.concatenate([rows, rows], axis=1)
        for plane in range(packing):
            half = 0.5 * jnp.dot(rows, weights[plane], preferred_element_type=f32) + half_bias
            hidden = (half + half * jnp.tanh(half)).astype(bf16)
            made = jnp.dot(hidden, second_ref[...], preferred_element_type=f32).astype(bf16)
            features[:, plane] = made.reshape(group, packed, width)
        for part in range(group // chunk):
            pieces = []
            for pair in range(part * chunk // 2, (part + 1) * chunk // 2):
                even = cells_got[base + 2 * pair]
                odd = cells_got[base + 2 * pair + 1]
                pieces += [even[0:1], jnp.where(lane < 64, even[1:2], odd[0:1]), odd[1:2]]
            cell = jnp.concatenate(pieces, axis=1)
            span = chunk * capacity
            spots = lax.broadcasted_iota(i32, (tile_cells, span), 0)
            onehot = jnp.where(spots == cell, 1.0, 0.0).astype(bf16)
            sums[...] += jnp.dot(
                onehot, features[pl.ds(part * chunk, chunk)].reshape(span, width), preferred_element_type=f32)
            line = lax.shift_right_arithmetic(cell * 1366, 16)
            column = cell - line * TILE_COLS
            lines = jnp.where(lax.broadcasted_iota(i32, (32, span), 0) == line, 1.0, 0.0).astype(bf16)
            columns = jnp.where(
                (lax.broadcasted_iota(i32, (TILE_COLS, span), 0) == column) & (cell >= 0), 1.0, 0.0).astype(bf16)
            counts[...] += lax.dot_general(columns, lines, (((1,), (1,)), ((), ())), preferred_element_type=f32)
        return 0

    lax.fori_loop(0, shards // group, work, 0)

    scale = 1.0 / jnp.maximum(counts[...], 1.0)
    for copy in kernels:
        copy.wait()
    encode_tile(sums, scale, first_kernel, second_kernel, conv_bias_ref, out_ref, field, shifted, middle,
                column_stage, row_edges, column_edges, corner_edges, row_halos, column_halos, corner_halos, send_halo, recv_halo)

    def drain(step, _):
        for copy in copies(step):
            copy.wait_send()
        return 0

    lax.fori_loop(1, shards, drain, 0)


def exchange(observations, destinations, cells, first_weight, first_bias, second_weight, conv_first, conv_bias,
             conv_second, shards, capacity, group=16, chunk=4):
    count_rows, values = observations.shape
    width = second_weight.shape[1]
    vmem = pl.BlockSpec(memory_space=pltpu.VMEM)
    anywhere = pl.BlockSpec(memory_space=pl.ANY)
    packing = 128 // values
    packed = capacity // packing
    lines = count_rows // 128
    field_rows = (TILE_ROWS + 5) * PITCH + 16
    dma = pltpu.SemaphoreType.DMA
    f32, bf16, i32 = jnp.float32, jnp.bfloat16, jnp.int32
    return pl.pallas_call(
        functools.partial(exchange_kernel, group, chunk),
        out_shape=jax.ShapeDtypeStruct((TILE_ROWS, TILE_COLS, width), bf16),
        in_specs=[anywhere, anywhere, anywhere, vmem, vmem, vmem, anywhere, vmem, anywhere],
        out_specs=vmem,
        scratch_shapes=[
            pltpu.VMEM((values, count_rows), f32),
            pltpu.VMEM((1, count_rows), i32),
            pltpu.VMEM((1, count_rows), i32),
            pltpu.VMEM((ROOM, 128), f32),
            pltpu.VMEM((ROOM + capacity, 128), f32),
            pltpu.VMEM((2 * shards, capacity), f32),
            pltpu.VMEM((2 * lines, 128), f32),
            pltpu.SMEM((lines, 128), i32),
            pltpu.VMEM((shards, 128), i32),
            pltpu.SMEM((shards, 128), i32),
            pltpu.VMEM((shards, packed, 128), bf16),
            pltpu.VMEM((shards, 2, 128), i32),
            pltpu.VMEM((shards, packed, 128), bf16),
            pltpu.VMEM((shards, 2, 128), i32),
            pltpu.VMEM((group, packing, packed, width), bf16),
            pltpu.VMEM((TILE_ROWS * TILE_COLS, width), f32),
            pltpu.VMEM((TILE_COLS, 32), f32),
            pltpu.VMEM((3, 3 * width, width), bf16),
            pltpu.VMEM((3, 3 * width, width), bf16),
            pltpu.VMEM((field_rows, width), f32),
            pltpu.VMEM((field_rows, 3 * width), bf16),
            pltpu.VMEM((field_rows, width), f32),
            pltpu.VMEM((2, 2, TILE_ROWS, width), f32),
            pltpu.VMEM((2, 2, TILE_COLS, width), bf16),
            pltpu.VMEM((2, 2, 32, width), bf16),
            pltpu.VMEM((2, 2, 4, width), f32),
            pltpu.VMEM((2, 2, TILE_COLS, width), bf16),
            pltpu.VMEM((2, 2, 32, width), bf16),
            pltpu.VMEM((2, 2, 4, width), f32),
            dma((5,)), dma((2,)), dma((shards,)), dma((shards,)), dma((shards,)), dma((shards,)),
            dma((8,)), dma((8,)),
        ],
        compiler_params=pltpu.CompilerParams(
            collective_id=0, has_side_effects=True, vmem_limit_bytes=56 * 1024 * 1024),
        name="exchange",
    )(observations.T, destinations.reshape(1, -1), cells.reshape(1, -1), first_weight, first_bias.reshape(1, -1),
      second_weight, conv_first.reshape(3, 3 * width, width), conv_bias.reshape(1, -1),
      conv_second.reshape(3, 3 * width, width))


def body(
    observations,
    destinations,
    cells,
    first_weight,
    first_bias,
    second_weight,
    conv_first,
    conv_bias,
    conv_second,
):
    shards = lax.axis_size("lat") * lax.axis_size("lon")
    capacity = 2 * observations.shape[0] // shards
    return exchange(observations, destinations, cells, first_weight, first_bias, second_weight, conv_first, conv_bias,
                    conv_second, shards, capacity)


def solution(mesh):
    in_specs = (
        P(("lat", "lon"), None),
        P(("lat", "lon"), None),
        P(("lat", "lon")),
        P(),
        P(),
        P(),
        P(),
        P(),
        P(),
    )
    out_specs = P("lat", "lon", None)
    return jax.shard_map(body, mesh=mesh, in_specs=in_specs, out_specs=out_specs, check_vma=False)
```

```python
import functools

import jax
import jax.numpy as jnp
from jax import lax
from jax.experimental import pallas as pl
from jax.experimental.pallas import tpu as pltpu
from jax.sharding import PartitionSpec as P

TILE_ROWS = 24
TILE_COLS = 48
BLOCK = 256
ROOM = 16384


PITCH = 64


def encode_tile(sums, scale, first_kernel, second_kernel, bias_ref, out_ref, field, shifted, middle,
                column_stage, row_edges, column_edges, corner_edges, row_halos, column_halos, corner_halos,
                send_halo, recv_halo):
    f32, bf16, i32 = jnp.float32, jnp.bfloat16, jnp.int32
    mesh_id = pl.DeviceIdType.MESH
    bands, sectors = lax.axis_size("lat"), lax.axis_size("lon")
    band, sector = lax.axis_index("lat"), lax.axis_index("lon")
    width = sums.shape[1]

    def at(line, column):
        return (line + 3) * PITCH + column

    north = band > 0
    south = band < bands - 1
    vertical = (
        (jnp.where(north, band - 1, 0), jnp.where(north, 0, sectors // 2), jnp.where(north, 1, 0)),
        (jnp.where(south, band + 1, bands - 1), jnp.where(south, 0, sectors // 2), jnp.where(south, 0, 1)),
    )
    copies = []

    def ship(source, target, slot, target_band, shift):
        copies.append(
            pltpu.make_async_remote_copy(
                src_ref=source, dst_ref=target, send_sem=send_halo.at[len(copies)], recv_sem=recv_halo.at[slot],
                device_id=(target_band, lax.rem(sector + shift + 2 * sectors, sectors)), device_id_type=mesh_id))
        copies[-1].start()

    def average(line):
        block = sums[pl.ds(line * TILE_COLS, TILE_COLS), :] * scale[:, line:line + 1]
        block = block.astype(bf16)
        field[pl.ds(at(line, 0), TILE_COLS), :] = block.astype(f32)
        return block

    ends = ((0, 1), (TILE_ROWS - 1, TILE_ROWS - 2))
    borders = ((0, 1), (TILE_COLS - 1, TILE_COLS - 2))
    for end, (target_band, shift, landing) in enumerate(vertical):
        for depth, line in enumerate(ends[end]):
            row_edges[end, depth] = average(line)
        ship(row_edges.at[end], row_halos.at[landing], landing, target_band, shift)
    for end, (target_band, shift, landing) in enumerate(vertical):
        for side, step in enumerate((-1, 1)):
            for i, line in enumerate(ends[end]):
                for j, column in enumerate(borders[side]):
                    corner_edges[end, side, pl.ds(2 * i + j, 1), :] = field[pl.ds(at(line, column), 1), :]
            ship(corner_edges.at[end, side], corner_halos.at[landing, 1 - side], 4 + 2 * landing + 1 - side,
                 target_band, shift + step)
    for line in range(2, TILE_ROWS - 2):
        average(line)
    blank = jnp.zeros((8, width), f32)
    for side, step in enumerate((-1, 1)):
        for depth, column in enumerate(borders[side]):
            for line in range(TILE_ROWS):
                column_stage[side, depth, pl.ds(line, 1), :] = field[pl.ds(at(line, column), 1), :]
            column_edges[side, depth] = jnp.concatenate([column_stage[side, depth], blank], axis=0).astype(bf16)
        ship(column_edges.at[side], column_halos.at[1 - side], 2 + 1 - side, band, step)
    arrivals = [row_halos.at[0], row_halos.at[1], column_halos.at[0], column_halos.at[1]]
    arrivals += [corner_halos.at[end, side] for end in range(2) for side in range(2)]
    for slot, buffer in enumerate(arrivals):
        pltpu.make_async_remote_copy(
            src_ref=buffer, dst_ref=buffer, send_sem=send_halo.at[slot], recv_sem=recv_halo.at[slot],
            device_id=(band, sector), device_id_type=mesh_id).wait_recv()

    for end, lines in enumerate(((-1, -2), (TILE_ROWS, TILE_ROWS + 1))):
        for depth, line in enumerate(lines):
            field[pl.ds(at(line, 0), TILE_COLS), :] = row_halos[end, depth].astype(f32)
    for side, columns in enumerate(((-1, -2), (TILE_COLS, TILE_COLS + 1))):
        for depth, column in enumerate(columns):
            column_stage[side, depth] = column_halos[side, depth].astype(f32)[:TILE_ROWS]
            for line in range(TILE_ROWS):
                field[pl.ds(at(line, column), 1), :] = column_stage[side, depth, pl.ds(line, 1), :]
        for end, lines in enumerate(((-1, -2), (TILE_ROWS, TILE_ROWS + 1))):
            for i, line in enumerate(lines):
                for j, column in enumerate(columns):
                    field[pl.ds(at(line, column), 1), :] = corner_halos[end, side, pl.ds(2 * i + j, 1), :]

    def spread(array, start, stop):
        for tap in range(3):
            shifted[pl.ds(start, stop - start), tap * width:(tap + 1) * width] = (
                array[pl.ds(start + tap - 1, stop - start), :].astype(bf16))

    low, high = at(-1, -16), at(TILE_ROWS, PITCH)
    spread(field, low - PITCH, high + PITCH)
    parts = [shifted[pl.ds(low + (tap - 1) * PITCH, high - low), :] for tap in range(3)]
    total = jnp.dot(jnp.concatenate(parts, axis=1), first_kernel[...].reshape(9 * width, width),
                    preferred_element_type=f32)
    tall = PITCH + 16
    turned = 0.0
    for tap in range(3):
        lines = jnp.concatenate(
            [shifted[pl.ds(at(line - (tap - 1), -16), tall), :] for line in (-1, TILE_ROWS)], axis=0)
        turned += jnp.dot(lines, first_kernel[tap], preferred_element_type=f32)
    half_bias = 0.5 * bias_ref[...]

    def activate(value):
        half = 0.5 * value + half_bias
        return half + half * jnp.tanh(half)

    middle[pl.ds(low, high - low), :] = activate(total)
    turned = activate(turned)
    spot = lax.broadcasted_iota(i32, (tall, width), 0)
    inside = (spot >= 15) & (spot < 16 + TILE_COLS + 1)
    for index, (line, polar) in enumerate(((-1, band == 0), (TILE_ROWS, band == bands - 1))):
        place = pl.ds(at(line, -16), tall)
        chosen = jnp.where(polar, 1, 0)
        middle[place, :] = jnp.where(
            inside & (chosen == 1), turned[index * tall:(index + 1) * tall], middle[place, :])

    start, stop = at(0, 0), at(TILE_ROWS, 0)
    spread(middle, start - PITCH, stop + PITCH)
    total = field[pl.ds(start, stop - start), :]
    parts = [shifted[pl.ds(start + (tap - 1) * PITCH, stop - start), :] for tap in range(3)]
    total += jnp.dot(jnp.concatenate(parts, axis=1), second_kernel[...].reshape(9 * width, width),
                     preferred_element_type=f32)
    out_ref[...] = total.reshape(TILE_ROWS, PITCH, width)[:, :TILE_COLS].astype(bf16)
    for copy in copies:
        copy.wait_send()


def own_place():
    sector = lax.axis_index("lon")
    return lax.axis_index("lat"), lax.div(sector, 8), lax.rem(lax.div(sector, 2), 4), lax.rem(sector, 2)


def partner(step, own):
    own_band, own_x, own_y, own_core = own
    core = lax.rem(step, 2)
    along = lax.rem(lax.div(step, 2), 4)
    half = lax.rem(lax.div(step, 8), 2)
    turn = lax.rem(lax.div(step, 16), 4)
    last = lax.div(step, 64)
    to_x = lax.rem(own_x + along, 4)
    to_y = lax.rem(own_y + along + turn, 4)
    to_core = lax.rem(own_core + core, 2)
    to_band = lax.rem(own_band + along + 2 * half + last, 4)
    return to_band, to_x * 8 + to_y * 2 + to_core


def order_rows(shards, capacity, dest, cell, obs, waits, source, ordered, spots, table, order, order_smem,
               begins, begins_smem, copy_sem):
    values, count_rows = obs.shape
    packing = 128 // values
    f32, bf16, i32 = jnp.float32, jnp.bfloat16, jnp.int32
    lines = count_rows // 128
    span = 4 * BLOCK

    band, sector = partner(lax.broadcasted_iota(i32, (shards, 1), 0), own_place())
    owner = band * lax.axis_size("lon") + sector
    lane = lax.broadcasted_iota(i32, (BLOCK, BLOCK + 128), 1)
    row = lax.broadcasted_iota(i32, (BLOCK, BLOCK + 128), 0)
    earlier = jnp.where((row < lane) | (lane >= BLOCK), 1.0, 0.0).astype(bf16)
    value_lane = lax.broadcasted_iota(i32, (values, 128), 1)
    value_row = lax.broadcasted_iota(i32, (values, 128), 0)
    spread = jnp.where(lax.rem(value_lane, values) == value_row, 1.0, 0.0).astype(bf16)
    ranks = lax.broadcasted_iota(i32, (capacity, BLOCK), 0).astype(f32)
    high_lines = lax.broadcasted_iota(i32, (lines, BLOCK), 0)
    low_lines = lax.broadcasted_iota(i32, (128, BLOCK), 0)
    number_lane = lax.broadcasted_iota(i32, (1, BLOCK), 1).astype(f32)

    table[...] = jnp.zeros_like(table)
    order[...] = jnp.zeros_like(order)
    ordered[pl.ds(count_rows, capacity), :] = jnp.zeros((capacity, 128), f32)
    waits[0].wait()

    def count(step, total):
        at = pl.multiple_of(step * (count_rows // 32), count_rows // 32)
        for part in range(count_rows // 32 // 128):
            total += jnp.where(owner == dest[:, pl.ds(at + 128 * part, 128)], 1.0, 0.0)
        return total

    total = lax.fori_loop(0, 32, count, jnp.zeros((shards, 128), f32))
    below = lax.broadcasted_iota(i32, (shards, shards), 0) > lax.broadcasted_iota(i32, (shards, shards), 1)
    begin = jnp.dot(jnp.where(below, 1.0, 0.0).astype(bf16), total.astype(bf16), preferred_element_type=f32)
    begin = jnp.sum(begin, axis=1, keepdims=True)
    begins[...] = jnp.broadcast_to(jnp.clip(begin.astype(i32), 0, count_rows), begins.shape)
    begins_copy = pltpu.make_async_copy(begins, begins_smem, copy_sem.at[0])
    begins_copy.start()
    waits[1].wait()
    waits[2].wait()

    def place(step, carry):
        weights, ranked, highs, lows = [], [], [], []
        for part in range(span // BLOCK):
            at = pl.multiple_of(step * span + part * BLOCK, BLOCK)
            named = jnp.where(owner == dest[:, pl.ds(at, BLOCK)], 1.0, 0.0)
            counted = jnp.dot(named.astype(bf16), earlier, preferred_element_type=f32)
            before = counted[:, :BLOCK] + jnp.concatenate([carry] * (BLOCK // 128), axis=1)
            carry = carry + counted[:, BLOCK:]
            rank = jnp.sum(named * before, axis=0, keepdims=True)
            spot = (rank + jnp.sum(named * begin, axis=0, keepdims=True)).astype(i32)
            cells = cell[:, pl.ds(at, BLOCK)]
            high = lax.shift_right_logical(cells, 6)
            low = cells - lax.shift_left(high, 6)
            weights.append(jnp.concatenate(
                [named * (high + 1).astype(f32), named * low.astype(f32)], axis=0).astype(bf16))
            ranked.append(jnp.where(ranks == rank, 1.0, 0.0).astype(bf16))
            spot_high = lax.shift_right_logical(spot, 7)
            spot_low = spot - lax.shift_left(spot_high, 7)
            here = high_lines == spot_high
            block_number = (step * (span // BLOCK) + part).astype(f32)
            highs.append(jnp.concatenate(
                [jnp.where(here, block_number, 0.0), jnp.where(here, number_lane, 0.0)], axis=0).astype(bf16))
            lows.append(jnp.where(low_lines == spot_low, 1.0, 0.0).astype(bf16))
            source[pl.ds(at, BLOCK), :] = lax.dot_general(
                obs[:, pl.ds(at, BLOCK)].astype(bf16), spread, (((0,), (0,)), ((), ())), preferred_element_type=f32)
        along = (((1,), (1,)), ((), ()))
        table[...] += lax.dot_general(
            jnp.concatenate(weights, axis=1), jnp.concatenate(ranked, axis=1), along, preferred_element_type=f32)
        order[...] += lax.dot_general(
            jnp.concatenate(highs, axis=1), jnp.concatenate(lows, axis=1), along, preferred_element_type=f32)
        return carry

    lax.fori_loop(0, count_rows // span, place, jnp.zeros((shards, 128), f32), unroll=12)

    numbers = order[:lines, :].astype(i32) * BLOCK + order[lines:, :].astype(i32)
    begins_copy.wait()
    begins[pl.ds(0, lines), :] = jnp.clip(numbers, 0, count_rows - 1)
    order_copy = pltpu.make_async_copy(begins.at[pl.ds(0, lines)], order_smem, copy_sem.at[1])
    order_copy.start()
    found = table[:shards, :].astype(i32) * 64 + table[shards:, :].astype(i32) - 64
    found = jnp.where(found >= 0, found, -1)
    absent = jnp.full((shards, 64), -1, i32)
    straight = jnp.concatenate([found, absent], axis=1)
    turned = jnp.concatenate([absent, found], axis=1)
    odd = lax.rem(lax.broadcasted_iota(i32, (shards, 1), 0), 2)
    placed = jnp.where(odd == 1, turned, straight)
    spots[:, 0, :] = placed[:, :128]
    spots[:, 1, :] = placed[:, 128:]
    order_copy.wait()


def exchange_kernel(group, chunk, obs_ref, dest_ref, cell_ref, first_ref, bias_ref, second_ref,
                    conv_first_ref, conv_bias_ref, conv_second_ref, out_ref,
                    obs, dest, cell, source, ordered, table, order, order_smem, begins, begins_smem,
                    outbox, spots, rows_got, cells_got, features, sums, counts, first_kernel, second_kernel,
                    field, shifted, middle,
                    column_stage, row_edges, column_edges, corner_edges, row_halos, column_halos, corner_halos, own_sem, copy_sem,
                    send_rows, send_cells, recv_rows, recv_cells, send_halo, recv_halo):
    shards, packed, _ = rows_got.shape
    values = first_ref.shape[0]
    width = second_ref.shape[1]
    packing = 128 // values
    capacity = packing * packed
    count_rows = obs.shape[1]
    tile_cells = TILE_ROWS * TILE_COLS
    f32, bf16, i32 = jnp.float32, jnp.bfloat16, jnp.int32
    mesh_id = pl.DeviceIdType.MESH

    barrier = pltpu.get_barrier_semaphore()
    loads = [
        pltpu.make_async_copy(source_ref, target, own_sem.at[number])
        for number, (source_ref, target) in enumerate((
            (dest_ref, dest), (cell_ref, cell), (obs_ref, obs), (conv_first_ref, first_kernel),
            (conv_second_ref, second_kernel)))
    ]
    for copy in loads:
        copy.start()
    kernels = loads[3:]

    band, sector = lax.axis_index("lat"), lax.axis_index("lon")
    bands = [lax.rem(band + shift, 4) for shift in range(4)]
    along_x = [8 * lax.rem(lax.div(sector, 8) + shift, 4) for shift in range(4)]
    along_y = [2 * lax.rem(lax.div(sector, 2) + shift, 4) for shift in range(4)]
    cores = [lax.rem(sector, 2), 1 - lax.rem(sector, 2)]
    for x in along_x:
        for y in along_y:
            for core in cores:
                place = x + y + core
                for to_band in bands:
                    if x is along_x[0] and y is along_y[0] and core is cores[0] and to_band is bands[0]:
                        continue
                    pl.semaphore_signal(barrier, inc=1, device_id=(to_band, place), device_id_type=mesh_id)

    order_rows(shards, capacity, dest, cell, obs, loads[:3], source, ordered, spots, table, order, order_smem,
               begins, begins_smem, copy_sem)
    pl.semaphore_wait(barrier, shards - 1)

    own = own_place()

    def copies(step):
        target = partner(step, own)
        return (
            pltpu.make_async_remote_copy(
                src_ref=outbox.at[step], dst_ref=rows_got.at[step], send_sem=send_rows.at[step],
                recv_sem=recv_rows.at[step], device_id=target, device_id_type=mesh_id),
            pltpu.make_async_remote_copy(
                src_ref=spots.at[step], dst_ref=cells_got.at[step], send_sem=send_cells.at[step],
                recv_sem=recv_cells.at[step], device_id=target, device_id_type=mesh_id),
        )

    plane_of = lax.broadcasted_iota(i32, (packed, 128), 1) // values

    def pack(step):
        begin = begins_smem[step, 0] & (ROOM - 1)
        rows = ordered[pl.ds(begin, packed), :]
        for plane in range(1, packing):
            rows = jnp.where(plane_of == plane, ordered[pl.ds(begin + plane * packed, packed), :], rows)
        return rows.astype(bf16)

    def send(step):
        outbox[step] = pack(step)
        for copy in copies(step):
            copy.start()

    pair = 2 * capacity

    def gather(turn, _):
        at = pl.multiple_of(turn * pair, pair)
        for line in range(pair // 128):
            for lane in range(128):
                number = order_smem[turn * (pair // 128) + line, lane]
                ordered[pl.ds(at + line * 128 + lane, 1), :] = source[pl.ds(number, 1), :]

        @pl.when(turn == 0)
        def _():
            rows_got[0] = pack(0)
            cells_got[0] = spots[0]

        @pl.when(turn > 0)
        def _():
            send(2 * turn)

        send(2 * turn + 1)
        return 0

    lax.fori_loop(0, count_rows // pair, gather, 0)

    def send_rest(turn, _):
        for part in range(4):
            send(4 * turn + part)
        return 0

    lax.fori_loop(count_rows // pair // 2, shards // 4, send_rest, 0)

    sums[...] = jnp.zeros_like(sums)
    counts[...] = jnp.zeros_like(counts)
    first = first_ref[...]
    first_high = first.astype(bf16)
    first_low = (first - first_high.astype(f32)).astype(bf16)
    blank = jnp.zeros((values, width), bf16)
    weights = []
    for plane in range(packing):
        pieces = [blank] * (2 * packing)
        pieces[plane] = first_high
        pieces[packing + plane] = first_low
        weights.append(jnp.concatenate(pieces, axis=0))
    half_bias = 0.5 * bias_ref[...]
    lane = lax.broadcasted_iota(i32, (1, 128), 1)

    def receive(step, _):
        for copy in copies(step):
            copy.wait_recv()
        return 0

    def work(number, _):
        base = number * group
        lax.fori_loop(jnp.maximum(base, 1), base + group, receive, 0)
        rows = rows_got[pl.ds(base, group)].reshape(group * packed, 128)
        rows = jnp.concatenate([rows, rows], axis=1)
        for plane in range(packing):
            half = 0.5 * jnp.dot(rows, weights[plane], preferred_element_type=f32) + half_bias
            hidden = (half + half * jnp.tanh(half)).astype(bf16)
            made = jnp.dot(hidden, second_ref[...], preferred_element_type=f32).astype(bf16)
            features[:, plane] = made.reshape(group, packed, width)
        for part in range(group // chunk):
            pieces = []
            for pair in range(part * chunk // 2, (part + 1) * chunk // 2):
                even = cells_got[base + 2 * pair]
                odd = cells_got[base + 2 * pair + 1]
                pieces += [even[0:1], jnp.where(lane < 64, even[1:2], odd[0:1]), odd[1:2]]
            cell = jnp.concatenate(pieces, axis=1)
            span = chunk * capacity
            spots = lax.broadcasted_iota(i32, (tile_cells, span), 0)
            onehot = jnp.where(spots == cell, 1.0, 0.0).astype(bf16)
            sums[...] += jnp.dot(
                onehot, features[pl.ds(part * chunk, chunk)].reshape(span, width), preferred_element_type=f32)
            line = lax.shift_right_arithmetic(cell * 1366, 16)
            column = cell - line * TILE_COLS
            lines = jnp.where(lax.broadcasted_iota(i32, (32, span), 0) == line, 1.0, 0.0).astype(bf16)
            columns = jnp.where(
                (lax.broadcasted_iota(i32, (TILE_COLS, span), 0) == column) & (cell >= 0), 1.0, 0.0).astype(bf16)
            counts[...] += lax.dot_general(columns, lines, (((1,), (1,)), ((), ())), preferred_element_type=f32)
        return 0

    lax.fori_loop(0, shards // group, work, 0)

    scale = 1.0 / jnp.maximum(counts[...], 1.0)
    for copy in kernels:
        copy.wait()
    encode_tile(sums, scale, first_kernel, second_kernel, conv_bias_ref, out_ref, field, shifted, middle,
                column_stage, row_edges, column_edges, corner_edges, row_halos, column_halos, corner_halos, send_halo, recv_halo)

    def drain(step, _):
        for copy in copies(step):
            copy.wait_send()
        return 0

    lax.fori_loop(1, shards, drain, 0)


def exchange(observations, destinations, cells, first_weight, first_bias, second_weight, conv_first, conv_bias,
             conv_second, shards, capacity, group=16, chunk=4):
    count_rows, values = observations.shape
    width = second_weight.shape[1]
    vmem = pl.BlockSpec(memory_space=pltpu.VMEM)
    anywhere = pl.BlockSpec(memory_space=pl.ANY)
    packing = 128 // values
    packed = capacity // packing
    lines = count_rows // 128
    field_rows = (TILE_ROWS + 5) * PITCH + 16
    dma = pltpu.SemaphoreType.DMA
    f32, bf16, i32 = jnp.float32, jnp.bfloat16, jnp.int32
    return pl.pallas_call(
        functools.partial(exchange_kernel, group, chunk),
        out_shape=jax.ShapeDtypeStruct((TILE_ROWS, TILE_COLS, width), bf16),
        in_specs=[anywhere, anywhere, anywhere, vmem, vmem, vmem, anywhere, vmem, anywhere],
        out_specs=vmem,
        scratch_shapes=[
            pltpu.VMEM((values, count_rows), f32),
            pltpu.VMEM((1, count_rows), i32),
            pltpu.VMEM((1, count_rows), i32),
            pltpu.VMEM((ROOM, 128), f32),
            pltpu.VMEM((ROOM + capacity, 128), f32),
            pltpu.VMEM((2 * shards, capacity), f32),
            pltpu.VMEM((2 * lines, 128), f32),
            pltpu.SMEM((lines, 128), i32),
            pltpu.VMEM((shards, 128), i32),
            pltpu.SMEM((shards, 128), i32),
            pltpu.VMEM((shards, packed, 128), bf16),
            pltpu.VMEM((shards, 2, 128), i32),
            pltpu.VMEM((shards, packed, 128), bf16),
            pltpu.VMEM((shards, 2, 128), i32),
            pltpu.VMEM((group, packing, packed, width), bf16),
            pltpu.VMEM((TILE_ROWS * TILE_COLS, width), f32),
            pltpu.VMEM((TILE_COLS, 32), f32),
            pltpu.VMEM((3, 3 * width, width), bf16),
            pltpu.VMEM((3, 3 * width, width), bf16),
            pltpu.VMEM((field_rows, width), f32),
            pltpu.VMEM((field_rows, 3 * width), bf16),
            pltpu.VMEM((field_rows, width), f32),
            pltpu.VMEM((2, 2, TILE_ROWS, width), f32),
            pltpu.VMEM((2, 2, TILE_COLS, width), bf16),
            pltpu.VMEM((2, 2, 32, width), bf16),
            pltpu.VMEM((2, 2, 4, width), f32),
            pltpu.VMEM((2, 2, TILE_COLS, width), bf16),
            pltpu.VMEM((2, 2, 32, width), bf16),
            pltpu.VMEM((2, 2, 4, width), f32),
            dma((5,)), dma((2,)), dma((shards,)), dma((shards,)), dma((shards,)), dma((shards,)),
            dma((8,)), dma((8,)),
        ],
        compiler_params=pltpu.CompilerParams(
            collective_id=0, has_side_effects=True, vmem_limit_bytes=56 * 1024 * 1024),
        name="exchange",
    )(observations.T, destinations.reshape(1, -1), cells.reshape(1, -1), first_weight, first_bias.reshape(1, -1),
      second_weight, conv_first.reshape(3, 3 * width, width), conv_bias.reshape(1, -1),
      conv_second.reshape(3, 3 * width, width))


def body(
    observations,
    destinations,
    cells,
    first_weight,
    first_bias,
    second_weight,
    conv_first,
    conv_bias,
    conv_second,
):
    shards = lax.axis_size("lat") * lax.axis_size("lon")
    capacity = 2 * observations.shape[0] // shards
    return exchange(observations, destinations, cells, first_weight, first_bias, second_weight, conv_first, conv_bias,
                    conv_second, shards, capacity)


def solution(mesh):
    in_specs = (
        P(("lat", "lon"), None),
        P(("lat", "lon"), None),
        P(("lat", "lon")),
        P(),
        P(),
        P(),
        P(),
        P(),
        P(),
    )
    out_specs = P("lat", "lon", None)
    return jax.shard_map(body, mesh=mesh, in_specs=in_specs, out_specs=out_specs, check_vma=False)
```
